128 devices in a mesh: sec: 4 (over y), brick: 32 (over x, z, core).
Axes of the slice: x: 4, y: 4, z: 4, core: 2. Of those that a mesh axis runs over, the one named last changes fastest.
Arguments:
- melt: float32 [64, 16, 7, 512], P('brick', None, None, 'sec'), may hold values from -6 to 6
- grain_velocity: float32 [32768, 3, 128], P(('sec', 'brick')), may hold values from -6 to 6
- grain_radius: float32 [32768, 128], P(('sec', 'brick')), may hold values from 0.5 to 2
- parcel_cell: int32 [32768, 128], P(('sec', 'brick')), may hold values from 0 to 4095
- target_brick: int32 [32768], P(('sec', 'brick')), may hold values from 0 to 127, as said below
- block_count: int32 [32768], P(('sec', 'brick')), may hold values from 64 to 128
- slope: float32 [3], replicated, may hold values from -2 to -0.5
- partition: float32 [3], replicated, may hold values from 0.1 to 0.9
- diffusivity: float32 [7], replicated, may hold values from 0.08 to 0.16
Outputs:
- melt_out: float32 [64, 16, 7, 512], P('brick', None, None, 'sec')
- velocity_out: float32 [32768, 3, 128], P(('sec', 'brick'))
- radius_out: float32 [32768, 128], P(('sec', 'brick'))
The draws below stay inside these ranges and needn't reach their ends.
Inputs may be any that keep to these rules, and one draw needn't show every extreme that they name: `target_brick`: each device's 256 blocks name at most 4 blocks for any one brick; in every draw one brick, the same for all devices, is named by exactly 4 blocks of every device. The live parcels of a block are its first block_count slots.
All inputs are finite; a program needn't handle non-finite values.
Results may differ from the reference program's by a relative error of at most 0.0003.
The reference program's roundings to bfloat16 on the way (of `sources`) count: a program that leaves them out, or rounds other values in their place, can miss the bound.
Values sent between devices are 32-bit elements; how exact they have to be, the bound alone decides.
No kernel may reach another device: no remote copies, remote signals or barrier semaphores. Data moves between devices by JAX's collectives and lax.ppermute only.
A program may use at most 64 MiB of HBM per device.

```python
import math
import jax
import jax.numpy as jnp

SOLUTES = 3
BX = 2
BY = 16
BZ = 128
BS = 128
NBLK = 256
ITERS = 2
CAP = 4
NX = 64
NY = 16
NZ = 512
BLOCKS = 32768
N_BRICK = 32
DEVICES = 128


def draw_target_brick(key, part):
    hot = jax.random.randint(jax.random.fold_in(key, 7), (), 0, DEVICES)

    def one_device(device):
        sub = jax.random.fold_in(key, device)
        others = (hot + 1 + jnp.arange(DEVICES - 1, dtype=jnp.int32)) % DEVICES
        pool = jnp.repeat(others, CAP)
        picks = jax.random.permutation(sub, pool)[:NBLK - CAP]
        rows = jnp.concatenate([jnp.full((CAP,), hot, jnp.int32), picks.astype(jnp.int32)])
        return jax.random.permutation(jax.random.fold_in(sub, 1), rows)
    return jax.vmap(one_device)(jnp.arange(DEVICES, dtype=jnp.int32)).reshape(-1).astype(jnp.int32)


def plant(drawn, rng, least, high):
    dims = drawn.shape
    index_at = [jax.random.randint(jax.random.fold_in(rng, axis), (), 0, dims[axis]) for axis in range(len(dims))]
    drawn = drawn.at[tuple(index_at)].set(least)
    longest = dims.index(max(dims))
    index_at[longest] = (index_at[longest] + 1) % dims[longest]
    return drawn.at[tuple(index_at)].set(high)


def steps_of(key, shape, pieces, least, high):
    loudness = 1.0
    for axis_at, parts in pieces:
        steps = jax.random.uniform(jax.random.fold_in(jax.random.fold_in(key, 6), axis_at), (parts,), jnp.float32, least / len(pieces), high / len(pieces))
        loudness = loudness * jnp.repeat(jnp.exp(steps), shape[axis_at] // parts).reshape((-1,) + (1,) * (len(shape) - 1 - axis_at))
    return loudness


def normal_values(own_key, shape, width, limit, pieces=(), kind=jnp.bfloat16):
    entries = jax.random.normal(own_key, shape, jnp.float32) * width
    if len(pieces) > 0:
        entries = steps_of(own_key, shape, pieces, -0.22, 0.18) * entries
    return jnp.clip(entries, min=-limit, max=limit).astype(kind)


def setup_inputs(seed: int = 0) -> dict:
    streams_of = jax.random.split(jax.random.key(seed), 10)
    melt = normal_values(streams_of[0], (NX, NY, 4 + SOLUTES, NZ), 1.0, 6.0, ((0, 32), (3, 4)), jnp.float32)
    grain_velocity = normal_values(streams_of[1], (BLOCKS, 3, BS), 1.0, 6.0, ((0, 128),), jnp.float32)
    grain_radius = jnp.clip(jnp.exp(math.log(2.0) - 1.3862944 * jax.random.uniform(streams_of[2], (BLOCKS, BS), jnp.float32) ** steps_of(streams_of[2], (BLOCKS, BS), ((0, 128),), -0.2, 0.2)), 0.5, 2.0)
    parcel_cell = plant(jax.random.randint(streams_of[3], (BLOCKS, BS), 0, BX * BY * BZ), jax.random.fold_in(streams_of[3], 1), 0, (BX * BY * BZ) - 1).astype(jnp.int32)
    target_brick = draw_target_brick(jax.random.fold_in(streams_of[9], 71), 0)
    block_count = plant(jax.random.randint(streams_of[5], (BLOCKS,), BS // 2, BS + 1), jax.random.fold_in(streams_of[5], 1), BS // 2, BS).astype(jnp.int32)
    slope = jnp.clip(jax.random.uniform(streams_of[6], (SOLUTES,), jnp.float32, -2.0, -0.5), -2.0, -0.5)
    partition = jnp.clip(jax.random.uniform(streams_of[7], (SOLUTES,), jnp.float32, 0.1, 0.9), 0.1, 0.9)
    diffusivity = jnp.clip(jax.random.uniform(streams_of[8], (4 + SOLUTES,), jnp.float32, 0.08, 0.16), 0.08, 0.16)
    return {"melt": melt, "grain_velocity": grain_velocity, "grain_radius": grain_radius, "parcel_cell": parcel_cell, "target_brick": target_brick, "block_count": block_count, "slope": slope, "partition": partition, "diffusivity": diffusivity}


GROW = 0.4
DRAG = 0.25
MOMENT = 0.4
LATENT = 0.5
SETTLE = 0.1


def grain_physics(probe, velocity, radius, slope, partition):
    flow = probe[..., 0:3]
    temper = probe[..., 3]
    concen = probe[..., 4:]
    under = jnp.sum(concen * slope, axis=-1) - temper
    growth = GROW * jax.nn.softplus(under)
    beta = DRAG / (radius * radius)
    slip = flow - velocity
    momentum = -(MOMENT * radius * radius * radius * beta)[..., None] * slip
    heat = LATENT * growth * radius
    solute = (1.0 - partition) * concen * (growth * radius)[..., None]
    sources = jnp.concatenate([momentum, heat[..., None], solute], axis=-1)
    settle = jnp.array([0.0, 0.0, SETTLE], jnp.float32)
    new_velocity = velocity + beta[..., None] * slip - settle * radius[..., None]
    new_radius = radius + growth / radius
    return sources, new_velocity, new_radius


def diffuse(melt, diffusivity):
    padded = jnp.pad(melt, ((1, 1), (1, 1), (0, 0), (1, 1)))
    beside = padded[2:, 1:-1, :, 1:-1] + padded[:-2, 1:-1, :, 1:-1]
    beside = beside + padded[1:-1, 2:, :, 1:-1] + padded[1:-1, :-2, :, 1:-1]
    beside = beside + padded[1:-1, 1:-1, :, 2:] + padded[1:-1, 1:-1, :, :-2]
    return melt + diffusivity[None, None, :, None] * (beside - 6.0 * melt)


def reference(melt, grain_velocity, grain_radius, parcel_cell, target_brick, block_count, slope, partition, diffusivity):
    comps = melt.shape[2]
    slots = jnp.arange(BS, dtype=jnp.int32)
    live = slots[None, :] < block_count[:, None]
    brick_of = (target_brick % N_BRICK)[:, None]
    level_of = (target_brick // N_BRICK)[:, None]
    gx = brick_of * BX + parcel_cell // (BY * BZ)
    gy = (parcel_cell // BZ) % BY
    gz = level_of * BZ + parcel_cell % BZ
    flat = ((gx * NY + gy) * NZ + gz).astype(jnp.int32)
    velocity = jnp.transpose(grain_velocity, (0, 2, 1))
    radius = grain_radius
    for step in range(ITERS):
        lowered = melt.astype(jnp.bfloat16)
        table = jnp.transpose(lowered, (0, 1, 3, 2)).reshape(NX * NY * NZ, comps)
        probe = table[flat].astype(jnp.float32)
        sources, new_velocity, new_radius = grain_physics(probe, velocity, radius, slope, partition)
        sources = jnp.where(live[..., None], sources, 0.0).astype(jnp.bfloat16)
        deposit = jax.ops.segment_sum(sources.astype(jnp.float32).reshape(-1, comps), flat.reshape(-1), num_segments=NX * NY * NZ)
        deposit = jnp.transpose(deposit.reshape(NX, NY, NZ, comps), (0, 1, 3, 2))
        velocity = jnp.where(live[..., None], new_velocity, velocity)
        radius = jnp.where(live, new_radius, radius)
        melt = diffuse(melt, diffusivity) + deposit
    return melt, jnp.transpose(velocity, (0, 2, 1)), radius
```

```python
import jax
import jax.numpy as jnp
from jax import lax
from jax.experimental import pallas as pl
from jax.experimental.pallas import tpu as pltpu
from jax.sharding import PartitionSpec as P

AXES = ("sec", "brick")
CAP = 4
LANES = 128
COMPS = 7
SEND = 5
BACK = 4
GROUP = 8

GROW = 0.4
DRAG = 0.25
MOMENT = 0.4
LATENT = 0.5
SETTLE = 0.1

VMEM = pl.BlockSpec(memory_space=pltpu.VMEM)
SMEM = pl.BlockSpec(memory_space=pltpu.SMEM)
LIMIT = 48 * 2**20


def pack_kernel(target, count, velo, radi, cell, sent, slot_of, seen):
    blocks = radi.shape[0]
    bricks = seen.shape[0]
    sent[...] = jnp.full(sent.shape, -1.0, jnp.float32)
    lane = lax.broadcasted_iota(jnp.int32, (1, LANES), 1)

    def clear(i, _):
        seen[i] = 0
        return 0

    lax.fori_loop(0, bricks, clear, 0, unroll=8)

    def place(k, _):
        brick = target[k]
        rank = seen[brick]
        seen[brick] = rank + 1
        slot = brick * CAP + rank
        slot_of[k] = slot
        row = slot * SEND
        for c in range(3):
            sent[pl.ds(row + c, 1), :] = velo[k, pl.ds(c, 1), :]
        sent[pl.ds(row + 3, 1), :] = radi[pl.ds(k, 1), :]
        where = cell[pl.ds(k, 1), :].astype(jnp.float32)
        sent[pl.ds(row + 4, 1), :] = jnp.where(lane < count[k], where, -1.0)
        return 0

    lax.fori_loop(0, blocks, place, 0, unroll=4)


def unpack_kernel(slot_of, back, velo, radi):
    blocks = radi.shape[0]

    def place(k, _):
        row = slot_of[k] * BACK
        for c in range(3):
            velo[k, pl.ds(c, 1), :] = back[pl.ds(row + c, 1), :]
        radi[pl.ds(k, 1), :] = back[pl.ds(row + 3, 1), :]
        return 0

    lax.fori_loop(0, blocks, place, 0, unroll=4)


def diffused(melt, low_x, high_x, low_z, high_z, rate):
    rows, size_z = melt.shape
    size_y = low_x.shape[0]
    lane = lax.broadcasted_iota(jnp.int32, (rows, size_z), 1)
    level = lax.broadcasted_iota(jnp.int32, (rows, size_z), 0) % size_y
    below_x = jnp.concatenate([low_x, melt[:-size_y]], axis=0)
    above_x = jnp.concatenate([melt[size_y:], high_x], axis=0)
    below_y = jnp.where(level == 0, 0.0, pltpu.roll(melt, 1, 0))
    above_y = jnp.where(level == size_y - 1, 0.0, pltpu.roll(melt, rows - 1, 0))
    below_z = jnp.where(lane == 0, low_z, pltpu.roll(melt, 1, 1))
    above_z = jnp.where(lane == size_z - 1, high_z, pltpu.roll(melt, size_z - 1, 1))
    beside = above_x + below_x + above_y + below_y + above_z + below_z
    return melt + rate * (beside - 6.0 * melt)


def deposit_of(acc, comp, size_x, size_y):
    part = acc[comp * size_y : (comp + 1) * size_y, :]
    size_z = part.shape[1] // size_x
    return jnp.concatenate(
        [part[:, x * size_z : (x + 1) * size_z] for x in range(size_x)], axis=0
    )


def steps_kernel(
    slope, partition, rate, got, melt, low_x, high_x, low_z, high_z, back, melt_mid, acc, table
):
    size_y = low_x.shape[1]
    columns = melt.shape[1]
    size_z = melt.shape[2]
    size_x = columns // size_y
    groups = got.shape[0] // (SEND * GROUP)
    row_iota = lax.broadcasted_iota(jnp.int32, (size_x * size_z, LANES), 0)
    y_iota = lax.broadcasted_iota(jnp.int32, (size_y, LANES), 0)

    def one_step(first):
        acc[...] = jnp.zeros_like(acc)

        def group(g, _):
            def rows(field):
                if first:
                    return got[pl.ds(g * (SEND * GROUP) + field, GROUP, stride=SEND), :]
                return back[pl.ds(g * (BACK * GROUP) + field, GROUP, stride=BACK), :]

            cell = got[pl.ds(g * (SEND * GROUP) + 4, GROUP, stride=SEND), :].astype(jnp.int32)
            live = cell >= 0
            z = cell & (size_z - 1)
            column = cell >> 7
            probe = [jnp.zeros((GROUP, LANES), jnp.float32)] * COMPS
            for j in range(columns):
                here = column == j
                for c in range(COMPS):
                    line = jnp.broadcast_to(table[c, j : j + 1, :], (GROUP, LANES))
                    picked = jnp.take_along_axis(line, z, axis=1)
                    probe[c] = jnp.where(here, picked, probe[c])
            velo = [rows(0), rows(1), rows(2)]
            radi = rows(3)
            under = (
                probe[4] * slope[0] + probe[5] * slope[1] + probe[6] * slope[2]
            ) - probe[3]
            growth = GROW * (jnp.maximum(under, 0.0) + jnp.log1p(jnp.exp(-jnp.abs(under))))
            beta = DRAG / (radi * radi)
            push = -(MOMENT * radi * radi * radi * beta)
            slip = [probe[c] - velo[c] for c in range(3)]
            fed = growth * radi
            sources = [push * slip[c] for c in range(3)] + [LATENT * growth * radi]
            sources += [(1.0 - partition[s]) * probe[4 + s] * fed for s in range(3)]
            new_velo = [velo[c] + beta * slip[c] for c in range(3)]
            new_velo[2] = new_velo[2] - SETTLE * radi
            new_radi = radi + growth / radi
            base = g * (BACK * GROUP)
            for c in range(3):
                back[pl.ds(base + c, GROUP, stride=BACK), :] = jnp.where(live, new_velo[c], velo[c])
            back[pl.ds(base + 3, GROUP, stride=BACK), :] = jnp.where(live, new_radi, radi)
            y = jnp.where(live, column & (size_y - 1), size_y)
            line = ((column >> 4) * size_z) | z
            lefts, rights = [], []
            for b in range(GROUP):
                mask = y_iota == y[b : b + 1, :]
                lefts.append(
                    jnp.concatenate(
                        [jnp.where(mask, s[b : b + 1, :], 0.0).astype(jnp.bfloat16) for s in sources],
                        axis=0,
                    )
                )
                rights.append((row_iota == line[b : b + 1, :]).astype(jnp.bfloat16))
            left = jnp.concatenate(lefts, axis=1)
            right = jnp.concatenate(rights, axis=1)
            acc[...] += lax.dot_general(
                left, right, (((1,), (1,)), ((), ())), preferred_element_type=jnp.float32
            )
            return 0

        lax.fori_loop(0, groups, group, 0)

    table[...] = melt[...].astype(jnp.bfloat16).astype(jnp.float32)
    one_step(True)
    for c in range(COMPS):
        fresh = diffused(melt[c], low_x[c], high_x[c], low_z[c], high_z[c], rate[c])
        fresh = fresh + deposit_of(acc, c, size_x, size_y)
        melt_mid[c] = fresh
        table[c] = fresh.astype(jnp.bfloat16).astype(jnp.float32)
    one_step(False)


def finish_kernel(rate, melt, acc, low_x, high_x, low_z, high_z, out):
    size_y = low_x.shape[1]
    size_x = melt.shape[1] // size_y
    for c in range(COMPS):
        fresh = diffused(melt[c], low_x[c], high_x[c], low_z[c], high_z[c], rate[c])
        out[c] = fresh + deposit_of(acc, c, size_x, size_y)


def kernel_call(kernel, outs, in_specs, out_specs, scratch=()):
    return pl.pallas_call(
        kernel,
        out_shape=outs,
        in_specs=in_specs,
        out_specs=out_specs,
        scratch_shapes=list(scratch),
        compiler_params=pltpu.CompilerParams(vmem_limit_bytes=LIMIT),
    )


def shape(*dims):
    return jax.ShapeDtypeStruct(dims, jnp.float32)


def neighbours(melt, size_y):
    def shift(edge, axis, step):
        n = lax.axis_size(axis)
        return lax.ppermute(edge, axis, [(i, i + step) for i in range(n) if 0 <= i + step < n])

    low_x = shift(melt[:, -size_y:, :], "brick", 1)
    high_x = shift(melt[:, :size_y, :], "brick", -1)
    low_z = shift(melt[:, :, -1], "sec", 1)[:, :, None]
    high_z = shift(melt[:, :, 0], "sec", -1)[:, :, None]
    return low_x, high_x, low_z, high_z


def run_steps(got, melt, halo, slope, partition, rate, size_y):
    comps, columns, size_z = melt.shape
    size_x = columns // size_y
    slots = got.shape[0] // SEND
    return kernel_call(
        steps_kernel,
        (
            shape(slots * BACK, LANES),
            shape(comps, columns, size_z),
            shape(comps * size_y, size_x * size_z),
        ),
        [SMEM, SMEM, SMEM] + [VMEM] * 6,
        (VMEM, VMEM, VMEM),
        [pltpu.VMEM((comps, columns, size_z), jnp.float32)],
    )(slope, partition, rate, got, melt, *halo)


def exchange(rows, devices):
    each = rows.shape[0] // CAP
    swapped = lax.all_to_all(
        rows.reshape(each, CAP, LANES), AXES, split_axis=0, concat_axis=0, tiled=True
    )
    return swapped.reshape(rows.shape)


def local(melt, velocity, radius, cell, target, count, slope, partition, rate):
    devices = lax.axis_size(AXES)
    size_x, size_y, comps, size_z = melt.shape
    blocks = target.shape[0]
    slots = devices * CAP
    sent, slot_of = kernel_call(
        pack_kernel,
        (shape(slots * SEND, LANES), jax.ShapeDtypeStruct((blocks,), jnp.int32)),
        [SMEM, SMEM, VMEM, VMEM, VMEM],
        (VMEM, SMEM),
        [pltpu.SMEM((devices,), jnp.int32)],
    )(target, count, velocity, radius, cell)
    got = exchange(sent, devices)
    start = jnp.transpose(melt, (2, 0, 1, 3)).reshape(comps, size_x * size_y, size_z)
    halo = neighbours(start, size_y)
    back, middle, acc = run_steps(got, start, halo, slope, partition, rate, size_y)
    returned = exchange(back, devices)
    halo = neighbours(middle, size_y)
    final = kernel_call(
        finish_kernel,
        shape(comps, size_x * size_y, size_z),
        [SMEM] + [VMEM] * 6,
        VMEM,
    )(rate, middle, acc, *halo)
    melt_out = jnp.transpose(final.reshape(comps, size_x, size_y, size_z), (1, 2, 0, 3))
    velocity_out, radius_out = kernel_call(
        unpack_kernel,
        (shape(blocks, 3, LANES), shape(blocks, LANES)),
        [SMEM, VMEM],
        (VMEM, VMEM),
    )(slot_of, returned)
    return melt_out, velocity_out, radius_out


def solution(mesh):
    return jax.shard_map(
        local,
        mesh=mesh,
        in_specs=(
            P("brick", None, None, "sec"),
            P(AXES, None, None),
            P(AXES, None),
            P(AXES, None),
            P(AXES),
            P(AXES),
            P(),
            P(),
            P(),
        ),
        out_specs=(P("brick", None, None, "sec"), P(AXES, None, None), P(AXES, None)),
        check_vma=False,
    )
```

```python
import jax
import jax.numpy as jnp
from jax import lax
from jax.experimental import pallas as pl
from jax.experimental.pallas import tpu as pltpu
from jax.sharding import PartitionSpec as P

AXES = ("sec", "brick")
CAP = 4
LANES = 128
COMPS = 7
SEND = 5
BACK = 4
GROUP = 8
PAIRS = 3
TINY = 2.0**-126

GROW = 0.4
DRAG = 0.25
MOMENT = 0.4
LATENT = 0.5
SETTLE = 0.1

VMEM = pl.BlockSpec(memory_space=pltpu.VMEM)
SMEM = pl.BlockSpec(memory_space=pltpu.SMEM)
HBM = pl.BlockSpec(memory_space=pltpu.HBM)
LIMIT = 16 * 2**20
WHOLE = 64 * 2**20


def pack_kernel(
    target_hbm, count_hbm, velo_hbm, radi_hbm, cell_hbm,
    sent, slot_of, target, count, velo, radi, cell, seen, ready,
):
    blocks = radi.shape[0]
    bricks = seen.shape[0]
    pairs = [
        (target_hbm, target),
        (count_hbm, count),
        (velo_hbm, velo),
        (radi_hbm, radi),
        (cell_hbm, cell),
    ]
    copies = [
        pltpu.make_async_copy(source, into, ready.at[i]) for i, (source, into) in enumerate(pairs)
    ]
    for copy in copies:
        copy.start()

    def clear(i, _):
        seen[i] = 0
        return 0

    lax.fori_loop(0, bricks, clear, 0, unroll=16)
    sent[...] = jnp.full(sent.shape, -1.0, jnp.float32)
    lane = lax.broadcasted_iota(jnp.int32, (1, LANES), 1)
    copies[0].wait()

    def rank(k, _):
        brick = target[k]
        earlier = seen[brick]
        seen[brick] = earlier + 1
        slot_of[k] = brick * CAP + earlier
        return 0

    lax.fori_loop(0, blocks, rank, 0, unroll=16)
    for copy in copies[1:]:
        copy.wait()

    def place(k, _):
        row = slot_of[k] * SEND
        for c in range(3):
            sent[pl.ds(row + c, 1), :] = velo[c, pl.ds(k, 1), :]
        sent[pl.ds(row + 3, 1), :] = radi[pl.ds(k, 1), :]
        where = cell[pl.ds(k, 1), :].astype(jnp.float32)
        sent[pl.ds(row + 4, 1), :] = jnp.where(lane < count[k], where, -1.0)
        return 0

    lax.fori_loop(0, blocks, place, 0, unroll=8)


def unpack_kernel(slot_of, back, velo_hbm, radi_hbm, velo, radi, done):
    blocks = radi.shape[0]
    half = blocks // 2

    def place(k, _):
        row = slot_of[k] * BACK
        for c in range(3):
            velo[c, pl.ds(k, 1), :] = back[pl.ds(row + c, 1), :]
        radi[pl.ds(k, 1), :] = back[pl.ds(row + 3, 1), :]
        return 0

    copies = []
    for part in range(2):
        lax.fori_loop(part * half, (part + 1) * half, place, 0, unroll=8)
        own = pl.ds(part * half, half)
        copies += [
            pltpu.make_async_copy(velo.at[:, own], velo_hbm.at[:, own], done.at[2 * part]),
            pltpu.make_async_copy(radi.at[own], radi_hbm.at[own], done.at[2 * part + 1]),
        ]
        copies[-2].start()
        copies[-1].start()
    for copy in copies:
        copy.wait()


def diffused(melt, low_x, high_x, low_z, high_z, rate):
    rows, size_z = melt.shape
    size_y = low_x.shape[0]
    lane = lax.broadcasted_iota(jnp.int32, (rows, size_z), 1)
    level = lax.broadcasted_iota(jnp.int32, (rows, size_z), 0) % size_y
    below_x = jnp.concatenate([low_x, melt[:-size_y]], axis=0)
    above_x = jnp.concatenate([melt[size_y:], high_x], axis=0)
    below_y = jnp.where(level == 0, 0.0, pltpu.roll(melt, 1, 0))
    above_y = jnp.where(level == size_y - 1, 0.0, pltpu.roll(melt, rows - 1, 0))
    below_z = jnp.where(lane == 0, low_z, pltpu.roll(melt, 1, 1))
    above_z = jnp.where(lane == size_z - 1, high_z, pltpu.roll(melt, size_z - 1, 1))
    beside = above_x + below_x + above_y + below_y + above_z + below_z
    return melt + rate * (beside - 6.0 * melt)


def deposit_of(acc, comp, size_x, size_y):
    part = acc[comp * size_y : (comp + 1) * size_y, :]
    size_z = part.shape[1] // size_x
    return jnp.concatenate(
        [part[:, x * size_z : (x + 1) * size_z] for x in range(size_x)], axis=0
    )


def code_of(value):
    size = jnp.abs(value)
    exponent = jnp.floor(jnp.log2(jnp.maximum(size, TINY)))
    mantissa = size * power(-exponent)
    high = mantissa >= 2.0
    low = mantissa < 1.0
    exponent = jnp.where(high, exponent + 1.0, jnp.where(low, exponent - 1.0, exponent))
    mantissa = jnp.where(high, mantissa * 0.5, jnp.where(low, mantissa * 2.0, mantissa))
    code = (exponent + 126.0) * 128.0 + mantissa * 128.0
    code = jnp.where(size < TINY, 0.0, code)
    return jnp.where(value < 0.0, -code, code).astype(jnp.int32)


def value_of(code):
    size = jnp.abs(code)
    scale = power((size >> 7).astype(jnp.float32) - 127.0)
    value = ((size & 127) + 128).astype(jnp.float32) * (1.0 / 128.0) * scale
    value = jnp.where(size == 0, 0.0, value)
    return jnp.where(code < 0, -value, value)


def power(exponent):
    return jnp.exp2(exponent).astype(jnp.bfloat16).astype(jnp.float32)


def paired(high, low):
    return code_of(high) * 65536 + (code_of(low) & 65535)


def unpaired(found):
    first = [value_of(word >> 16) for word in found[:PAIRS]]
    second = [value_of((word << 16) >> 16) for word in found[:PAIRS]]
    return [*first, found[PAIRS], *second]


def steps_kernel(
    slope, partition, rate, got, melt, low_x, high_x, low_z, high_z, back, melt_mid, acc, table, plain, fed_rows
):
    size_y = low_x.shape[1]
    columns = melt.shape[1]
    size_z = melt.shape[2]
    size_x = columns // size_y
    groups = got.shape[0] // (SEND * GROUP)
    row_iota = lax.broadcasted_iota(jnp.int32, (size_x * size_z, LANES), 0)
    y_iota = lax.broadcasted_iota(jnp.int32, (size_y, LANES), 0)

    def one_step(first, *sums):

        def look(g):
            cell = got[pl.ds(g * (SEND * GROUP) + 4, GROUP, stride=SEND), :].astype(jnp.int32)
            z = cell & (size_z - 1)
            column = cell >> 7
            words = [jnp.zeros((GROUP, LANES), jnp.int32)] * PAIRS
            single = jnp.zeros((GROUP, LANES), jnp.float32)
            for j in range(columns):
                here = column == j
                for c in range(PAIRS):
                    row = jnp.broadcast_to(table[c, j : j + 1, :], (GROUP, LANES))
                    words[c] = jnp.where(here, jnp.take_along_axis(row, z, axis=1), words[c])
                row = jnp.broadcast_to(plain[j : j + 1, :], (GROUP, LANES))
                single = jnp.where(here, jnp.take_along_axis(row, z, axis=1), single)
            return (*words, single)

        def work(g, found):
            probe = unpaired(found)

            def rows(field):
                if first:
                    return got[pl.ds(g * (SEND * GROUP) + field, GROUP, stride=SEND), :]
                return back[pl.ds(g * (BACK * GROUP) + field, GROUP, stride=BACK), :]

            cell = got[pl.ds(g * (SEND * GROUP) + 4, GROUP, stride=SEND), :].astype(jnp.int32)
            live = cell >= 0
            z = cell & (size_z - 1)
            column = cell >> 7
            velo = [rows(0), rows(1), rows(2)]
            radi = rows(3)
            under = (
                probe[4] * slope[0] + probe[5] * slope[1] + probe[6] * slope[2]
            ) - probe[3]
            growth = GROW * (jnp.maximum(under, 0.0) + jnp.log1p(jnp.exp(-jnp.abs(under))))
            beta = DRAG / (radi * radi)
            push = -(MOMENT * radi * radi * radi * beta)
            slip = [probe[c] - velo[c] for c in range(3)]
            fed = growth * radi
            sources = [push * slip[c] for c in range(3)] + [LATENT * growth * radi]
            sources += [(1.0 - partition[s]) * probe[4 + s] * fed for s in range(3)]
            new_velo = [velo[c] + beta * slip[c] for c in range(3)]
            new_velo[2] = new_velo[2] - SETTLE * radi
            new_radi = radi + growth / radi
            base = g * (BACK * GROUP)
            for c in range(3):
                back[pl.ds(base + c, GROUP, stride=BACK), :] = jnp.where(live, new_velo[c], velo[c])
            back[pl.ds(base + 3, GROUP, stride=BACK), :] = jnp.where(live, new_radi, radi)
            for c in range(COMPS):
                fed_rows[c] = sources[c]

        def spend(g):
            cell = got[pl.ds(g * (SEND * GROUP) + 4, GROUP, stride=SEND), :].astype(jnp.int32)
            live = cell >= 0
            z = cell & (size_z - 1)
            column = cell >> 7
            y = jnp.where(live, column & (size_y - 1), size_y)
            line = ((column >> 4) * size_z) | z
            for t in range(GROUP // 2):
                lefts, rights = [], []
                for b in (2 * t, 2 * t + 1):
                    mask = y_iota == y[b : b + 1, :]
                    lefts.append(
                        jnp.concatenate(
                            [
                                jnp.where(mask, fed_rows[c, b : b + 1, :], 0.0).astype(jnp.bfloat16)
                                for c in range(COMPS)
                            ],
                            axis=0,
                        )
                    )
                    rights.append(jnp.where(row_iota == line[b : b + 1, :], 1.0, 0.0).astype(jnp.bfloat16))
                unit, stage = t % 2, t // 2
                pltpu.matmul_push_rhs(
                    jnp.concatenate(rights, axis=1),
                    staging_register=stage,
                    mxu_index=unit,
                    transpose=True,
                )
                pltpu.matmul_acc_lhs(
                    sums[unit], jnp.concatenate(lefts, axis=1), load_staged_rhs=stage
                )

        def group(g, probe):
            spend(g - 1)
            later = look(jnp.minimum(g + 1, groups - 1))
            work(g, probe)
            return later

        work(0, look(0))
        first_found = group(1, look(1))

        def two(i, found):
            return group(2 * i + 1, group(2 * i, found))

        lax.fori_loop(1, groups // 2, two, first_found)
        spend(groups - 1)
        acc[...] = pltpu.matmul_pop(sums[0]) + pltpu.matmul_pop(sums[1])

    def scoped(first):
        rows = acc.shape[0]
        width = acc.shape[1]
        pl.run_scoped(
            lambda *sums: one_step(first, *sums),
            pltpu.ACC(mxu_id=0)((rows, width), jnp.float32),
            pltpu.ACC(mxu_id=1)((rows, width), jnp.float32),
        )

    def fill(value):
        rounded = [value(c).astype(jnp.bfloat16).astype(jnp.float32) for c in range(COMPS)]
        for c in range(PAIRS):
            table[c] = paired(rounded[c], rounded[PAIRS + 1 + c])
        plain[...] = rounded[PAIRS]

    fill(lambda c: melt[c])
    scoped(True)
    for c in range(COMPS):
        fresh = diffused(melt[c], low_x[c], high_x[c], low_z[c], high_z[c], rate[c])
        fresh = fresh + deposit_of(acc, c, size_x, size_y)
        melt_mid[c] = fresh
    fill(lambda c: melt_mid[c])
    scoped(False)


def finish_kernel(rate, melt, acc, low_x, high_x, low_z, high_z, out):
    size_y = low_x.shape[1]
    size_x = melt.shape[1] // size_y
    for c in range(COMPS):
        fresh = diffused(melt[c], low_x[c], high_x[c], low_z[c], high_z[c], rate[c])
        out[c] = fresh + deposit_of(acc, c, size_x, size_y)


def kernel_call(kernel, outs, in_specs, out_specs, scratch=(), limit=LIMIT):
    return pl.pallas_call(
        kernel,
        out_shape=outs,
        in_specs=in_specs,
        out_specs=out_specs,
        scratch_shapes=list(scratch),
        compiler_params=pltpu.CompilerParams(vmem_limit_bytes=limit),
    )


def shape(*dims):
    return jax.ShapeDtypeStruct(dims, jnp.float32)


def neighbours(melt, size_y):
    def shift(edge, axis, step):
        n = lax.axis_size(axis)
        return lax.ppermute(edge, axis, [(i, i + step) for i in range(n) if 0 <= i + step < n])

    low_x = shift(melt[:, -size_y:, :], "brick", 1)
    high_x = shift(melt[:, :size_y, :], "brick", -1)
    low_z = shift(melt[:, :, -1], "sec", 1)[:, :, None]
    high_z = shift(melt[:, :, 0], "sec", -1)[:, :, None]
    return low_x, high_x, low_z, high_z


def run_steps(got, melt, halo, slope, partition, rate, size_y):
    comps, columns, size_z = melt.shape
    size_x = columns // size_y
    slots = got.shape[0] // SEND
    return kernel_call(
        steps_kernel,
        (
            shape(slots * BACK, LANES),
            shape(comps, columns, size_z),
            shape(comps * size_y, size_x * size_z),
        ),
        [SMEM, SMEM, SMEM] + [VMEM] * 6,
        (VMEM, VMEM, VMEM),
        [
            pltpu.VMEM((PAIRS, columns, size_z), jnp.int32),
            pltpu.VMEM((columns, size_z), jnp.float32),
            pltpu.VMEM((comps, GROUP, LANES), jnp.float32),
        ],
    )(slope, partition, rate, got, melt, *halo)


def exchange(rows, devices):
    each = rows.shape[0] // CAP
    swapped = lax.all_to_all(
        rows.reshape(each, CAP, LANES), AXES, split_axis=0, concat_axis=0, tiled=True
    )
    return swapped.reshape(rows.shape)


def local(melt, velocity, radius, cell, target, count, slope, partition, rate):
    devices = lax.axis_size(AXES)
    size_x, size_y, comps, size_z = melt.shape
    blocks = target.shape[0]
    slots = devices * CAP
    sent, slot_of = kernel_call(
        pack_kernel,
        (shape(slots * SEND, LANES), jax.ShapeDtypeStruct((blocks,), jnp.int32)),
        [HBM] * 5,
        (VMEM, SMEM),
        [
            pltpu.SMEM((blocks,), jnp.int32),
            pltpu.SMEM((blocks,), jnp.int32),
            pltpu.VMEM((3, blocks, LANES), jnp.float32),
            pltpu.VMEM((blocks, LANES), jnp.float32),
            pltpu.VMEM((blocks, LANES), jnp.int32),
            pltpu.SMEM((devices,), jnp.int32),
            pltpu.SemaphoreType.DMA((5,)),
        ],
        limit=WHOLE,
    )(target, count, jnp.transpose(velocity, (1, 0, 2)), radius, cell)
    got = exchange(sent, devices)
    start = jnp.transpose(melt, (2, 0, 1, 3)).reshape(comps, size_x * size_y, size_z)
    halo = neighbours(start, size_y)
    back, middle, acc = run_steps(got, start, halo, slope, partition, rate, size_y)
    returned = exchange(back, devices)
    halo = neighbours(middle, size_y)
    final = kernel_call(
        finish_kernel,
        shape(comps, size_x * size_y, size_z),
        [SMEM] + [VMEM] * 6,
        VMEM,
    )(rate, middle, acc, *halo)
    melt_out = jnp.transpose(final.reshape(comps, size_x, size_y, size_z), (1, 2, 0, 3))
    velocity_out, radius_out = kernel_call(
        unpack_kernel,
        (shape(3, blocks, LANES), shape(blocks, LANES)),
        [SMEM, VMEM],
        (HBM, HBM),
        [
            pltpu.VMEM((3, blocks, LANES), jnp.float32),
            pltpu.VMEM((blocks, LANES), jnp.float32),
            pltpu.SemaphoreType.DMA((4,)),
        ],
    )(slot_of, returned)
    return melt_out, jnp.transpose(velocity_out, (1, 0, 2)), radius_out


def solution(mesh):
    return jax.shard_map(
        local,
        mesh=mesh,
        in_specs=(
            P("brick", None, None, "sec"),
            P(AXES, None, None),
            P(AXES, None),
            P(AXES, None),
            P(AXES),
            P(AXES),
            P(),
            P(),
            P(),
        ),
        out_specs=(P("brick", None, None, "sec"), P(AXES, None, None), P(AXES, None)),
        check_vma=False,
    )
```

```python
import functools

import jax
import jax.numpy as jnp
from jax import lax
from jax.experimental import pallas as pl
from jax.experimental.pallas import tpu as pltpu
from jax.sharding import PartitionSpec as P

AXES = ("sec", "brick")
CAP = 4
LANES = 128
COMPS = 7
SEND = 5
BACK = 4
GROUP = 8
PAIRS = 3
TINY = 2.0**-126

GROW = 0.4
DRAG = 0.25
MOMENT = 0.4
LATENT = 0.5
SETTLE = 0.1

VMEM = pl.BlockSpec(memory_space=pltpu.VMEM)
SMEM = pl.BlockSpec(memory_space=pltpu.SMEM)
HBM = pl.BlockSpec(memory_space=pltpu.HBM)
LIMIT = 16 * 2**20
WHOLE = 64 * 2**20


def pack_kernel(
    target_hbm, count_hbm, velo_hbm, radi_hbm, cell_hbm,
    sent, slot_of, target, count, velo, radi, cell, seen, ready,
):
    blocks = radi.shape[0]
    bricks = seen.shape[0]
    pairs = [
        (target_hbm, target),
        (count_hbm, count),
        (velo_hbm, velo),
        (radi_hbm, radi),
        (cell_hbm, cell),
    ]
    copies = [
        pltpu.make_async_copy(source, into, ready.at[i]) for i, (source, into) in enumerate(pairs)
    ]
    for copy in copies:
        copy.start()

    def clear(i, _):
        seen[i] = 0
        return 0

    lax.fori_loop(0, bricks, clear, 0, unroll=16)
    sent[...] = jnp.full(sent.shape, -1.0, jnp.float32)
    lane = lax.broadcasted_iota(jnp.int32, (1, LANES), 1)
    copies[0].wait()

    def rank(k, _):
        brick = target[k]
        earlier = seen[brick]
        seen[brick] = earlier + 1
        slot_of[k] = brick * CAP + earlier
        return 0

    lax.fori_loop(0, blocks, rank, 0, unroll=16)
    for copy in copies[1:]:
        copy.wait()

    def place(k, _):
        row = slot_of[k] * SEND
        for c in range(3):
            sent[pl.ds(row + c, 1), :] = velo[c, pl.ds(k, 1), :]
        sent[pl.ds(row + 3, 1), :] = radi[pl.ds(k, 1), :]
        where = cell[pl.ds(k, 1), :].astype(jnp.float32)
        sent[pl.ds(row + 4, 1), :] = jnp.where(lane < count[k], where, -1.0)
        return 0

    lax.fori_loop(0, blocks, place, 0, unroll=8)


def unpack_kernel(slot_of, back, velo_hbm, radi_hbm, velo, radi, done):
    blocks = radi.shape[0]
    half = blocks // 2

    def place(k, _):
        row = slot_of[k] * BACK
        for c in range(3):
            velo[c, pl.ds(k, 1), :] = back[pl.ds(row + c, 1), :]
        radi[pl.ds(k, 1), :] = back[pl.ds(row + 3, 1), :]
        return 0

    copies = []
    for part in range(2):
        lax.fori_loop(part * half, (part + 1) * half, place, 0, unroll=8)
        own = pl.ds(part * half, half)
        copies += [
            pltpu.make_async_copy(velo.at[:, own], velo_hbm.at[:, own], done.at[2 * part]),
            pltpu.make_async_copy(radi.at[own], radi_hbm.at[own], done.at[2 * part + 1]),
        ]
        copies[-2].start()
        copies[-1].start()
    for copy in copies:
        copy.wait()


def diffused(melt, low_x, high_x, low_z, high_z, rate):
    rows, size_z = melt.shape
    size_y = low_x.shape[0]
    lane = lax.broadcasted_iota(jnp.int32, (rows, size_z), 1)
    level = lax.broadcasted_iota(jnp.int32, (rows, size_z), 0) % size_y
    below_x = jnp.concatenate([low_x, melt[:-size_y]], axis=0)
    above_x = jnp.concatenate([melt[size_y:], high_x], axis=0)
    below_y = jnp.where(level == 0, 0.0, pltpu.roll(melt, 1, 0))
    above_y = jnp.where(level == size_y - 1, 0.0, pltpu.roll(melt, rows - 1, 0))
    below_z = jnp.where(lane == 0, low_z, pltpu.roll(melt, 1, 1))
    above_z = jnp.where(lane == size_z - 1, high_z, pltpu.roll(melt, size_z - 1, 1))
    beside = above_x + below_x + above_y + below_y + above_z + below_z
    return melt + rate * (beside - 6.0 * melt)


def deposit_of(acc, comp, size_x, size_y):
    part = acc[comp * size_y : (comp + 1) * size_y, :]
    size_z = part.shape[1] // size_x
    return jnp.concatenate(
        [part[:, x * size_z : (x + 1) * size_z] for x in range(size_x)], axis=0
    )


def code_of(value):
    size = jnp.abs(value)
    exponent = jnp.floor(jnp.log2(jnp.maximum(size, TINY)))
    mantissa = size * power(-exponent)
    high = mantissa >= 2.0
    low = mantissa < 1.0
    exponent = jnp.where(high, exponent + 1.0, jnp.where(low, exponent - 1.0, exponent))
    mantissa = jnp.where(high, mantissa * 0.5, jnp.where(low, mantissa * 2.0, mantissa))
    code = (exponent + 126.0) * 128.0 + mantissa * 128.0
    code = jnp.where(size < TINY, 0.0, code)
    return jnp.where(value < 0.0, -code, code).astype(jnp.int32)


def value_of(code):
    size = jnp.abs(code)
    scale = power((size >> 7).astype(jnp.float32) - 127.0)
    value = ((size & 127) + 128).astype(jnp.float32) * (1.0 / 128.0) * scale
    value = jnp.where(size == 0, 0.0, value)
    return jnp.where(code < 0, -value, value)


def power(exponent):
    return jnp.exp2(exponent).astype(jnp.bfloat16).astype(jnp.float32)


def paired(high, low):
    return code_of(high) * 65536 + (code_of(low) & 65535)


def unpaired(found):
    first = [value_of(word >> 16) for word in found[:PAIRS]]
    second = [value_of((word << 16) >> 16) for word in found[:PAIRS]]
    return [*first, found[PAIRS], *second]


def spend_group(cell, fed_rows, dims, sums):
    size_x, size_y, size_z = dims
    row_iota = lax.broadcasted_iota(jnp.int32, (size_x * size_z, LANES), 0)
    y_iota = lax.broadcasted_iota(jnp.int32, (size_y, LANES), 0)
    z = cell & (size_z - 1)
    column = cell >> 7
    y = jnp.where(cell >= 0, column & (size_y - 1), size_y)
    line = ((column >> 4) * size_z) | z
    for t in range(GROUP // 2):
        lefts, rights = [], []
        for b in (2 * t, 2 * t + 1):
            mask = y_iota == y[b : b + 1, :]
            lefts.append(
                jnp.concatenate(
                    [
                        jnp.where(mask, fed_rows[c, b : b + 1, :], 0.0).astype(jnp.bfloat16)
                        for c in range(COMPS)
                    ],
                    axis=0,
                )
            )
            rights.append(
                jnp.where(row_iota == line[b : b + 1, :], 1.0, 0.0).astype(jnp.bfloat16)
            )
        unit, stage = t % 2, t // 2
        pltpu.matmul_push_rhs(
            jnp.concatenate(rights, axis=1),
            staging_register=stage,
            mxu_index=unit,
            transpose=True,
        )
        pltpu.matmul_acc_lhs(
            sums[unit], jnp.concatenate(lefts, axis=1), load_staged_rhs=stage
        )


def matrix_probe(cell, lines, dims, sums):
    size_x, size_y, size_z = dims
    row_iota = lax.broadcasted_iota(jnp.int32, (size_x * size_z, LANES), 0)
    y_iota = lax.broadcasted_iota(jnp.int32, (size_y, LANES), 0)
    column = cell >> 7
    y = jnp.where(cell >= 0, column & (size_y - 1), size_y)
    line = ((column >> 4) * size_z) | (cell & (size_z - 1))
    found = [[] for _ in range(COMPS)]
    for t in range(GROUP // 2):
        pair = (2 * t, 2 * t + 1)
        unit, stage = t % 2, t // 2
        pltpu.matmul_push_rhs(
            jnp.concatenate(
                [
                    jnp.where(row_iota == line[b : b + 1, :], 1.0, 0.0).astype(jnp.bfloat16)
                    for b in pair
                ],
                axis=1,
            ),
            staging_register=stage,
            mxu_index=unit,
        )
        pltpu.matmul_acc_lhs(sums[2 * stage + unit], lines[...], load_staged_rhs=stage)
        lifted = pltpu.matmul_pop(sums[2 * stage + unit])
        for i, b in enumerate(pair):
            mask = y_iota == y[b : b + 1, :]
            for c in range(COMPS):
                part = lifted[c * size_y : (c + 1) * size_y, i * LANES : (i + 1) * LANES]
                found[c].append(jnp.sum(jnp.where(mask, part, 0.0), axis=0, keepdims=True))
    return [jnp.concatenate(rows, axis=0) for rows in found]


def coupling_step(slope, partition, dims, refs, load_cell, load, store, span, sums, kept=None):
    size_x, size_y, size_z = dims
    table, plain, lines, fed_rows = refs
    columns = size_x * size_y

    def look(g):
        cell = load_cell(g)
        z = cell & (size_z - 1)
        column = cell >> 7
        words = [jnp.zeros((GROUP, LANES), jnp.int32)] * PAIRS
        single = jnp.zeros((GROUP, LANES), jnp.float32)
        for j in range(columns):
            here = column == j
            for c in range(PAIRS):
                row = jnp.broadcast_to(table[c, j : j + 1, :], (GROUP, LANES))
                words[c] = jnp.where(here, jnp.take_along_axis(row, z, axis=1), words[c])
            row = jnp.broadcast_to(plain[j : j + 1, :], (GROUP, LANES))
            single = jnp.where(here, jnp.take_along_axis(row, z, axis=1), single)
        return (*words, single)

    def work(g, probe, into):
        live = load_cell(g) >= 0
        velo = [load(g, 0), load(g, 1), load(g, 2)]
        radi = load(g, 3)
        under = (
            probe[4] * slope[0] + probe[5] * slope[1] + probe[6] * slope[2]
        ) - probe[3]
        growth = GROW * (jnp.maximum(under, 0.0) + jnp.log1p(jnp.exp(-jnp.abs(under))))
        beta = DRAG / (radi * radi)
        push = -(MOMENT * radi * radi * radi * beta)
        slip = [probe[c] - velo[c] for c in range(3)]
        fed = growth * radi
        sources = [push * slip[c] for c in range(3)] + [LATENT * growth * radi]
        sources += [(1.0 - partition[s]) * probe[4 + s] * fed for s in range(3)]
        new_velo = [velo[c] + beta * slip[c] for c in range(3)]
        new_velo[2] = new_velo[2] - SETTLE * radi
        new_radi = radi + growth / radi
        for c in range(3):
            store(g, c, jnp.where(live, new_velo[c], velo[c]))
        store(g, 3, jnp.where(live, new_radi, radi))
        for c in range(COMPS):
            into[c] = sources[c]

    def spend(g):
        spend_group(load_cell(g), fed_rows, dims, sums)

    first, stop = span
    last = stop - 1

    if kept is None:

        def group(g, found):
            spend(g - 1)
            later = look(jnp.minimum(g + 1, last))
            work(g, unpaired(found), fed_rows)
            return later

        def two(i, found):
            return group(2 * i + 1, group(2 * i, found))

        work(first, unpaired(look(first)), fed_rows)
        lax.fori_loop(first // 2 + 1, stop // 2, two, group(first + 1, look(first + 1)))
        spend(last)
    else:

        def pair(g):
            return look(g), tuple(matrix_probe(load_cell(g + 1), lines, dims, sums))

        def both(i, found):
            g = 2 * i
            later = pair(jnp.minimum(g + 2, last - 1))
            work(g, unpaired(found[0]), kept.at[g - first])
            work(g + 1, found[1], kept.at[g + 1 - first])
            return later

        def four(i, found):
            return both(2 * i + 1, both(2 * i, found))

        lax.fori_loop(first // 4, stop // 4, four, pair(first))


def deposit_scope(rows, width, body):
    pl.run_scoped(
        lambda *sums: body(sums),
        pltpu.ACC(mxu_id=0)((rows, width), jnp.float32),
        pltpu.ACC(mxu_id=1)((rows, width), jnp.float32),
    )


def fill_lines(lines, value, size_y):
    for c in range(COMPS):
        part = value(c).astype(jnp.bfloat16)
        lines[c * size_y : (c + 1) * size_y, :] = jnp.concatenate(
            [part[x : x + size_y] for x in range(0, part.shape[0], size_y)], axis=1
        )


def fill_table(table, plain, value):
    rounded = [value(c).astype(jnp.bfloat16).astype(jnp.float32) for c in range(COMPS)]
    for c in range(PAIRS):
        table[c] = paired(rounded[c], rounded[PAIRS + 1 + c])
    plain[...] = rounded[PAIRS]


def got_cell(got, g):
    return got[pl.ds(g * (SEND * GROUP) + 4, GROUP, stride=SEND), :].astype(jnp.int32)


def steps_kernel(
    slope, partition, rate, got, melt, low_x, high_x, low_z, high_z,
    back, melt_mid, acc, kept, *refs,
):
    table, plain, lines, _ = refs
    size_y = low_x.shape[1]
    size_x = melt.shape[1] // size_y
    dims = (size_x, size_y, melt.shape[2])
    groups = got.shape[0] // (SEND * GROUP)

    def stay(g, f):
        return pl.ds(g * (BACK * GROUP) + f, GROUP, stride=BACK)

    def store(g, f, value):
        back[stay(g, f), :] = value

    def step(load, share, kept):
        def body(sums):
            coupling_step(
                slope, partition, dims, refs, lambda g: got_cell(got, g), load, store,
                (share, groups), sums,
            )
            acc[...] = pltpu.matmul_pop(sums[0]) + pltpu.matmul_pop(sums[1])

        def keep(*sums):
            coupling_step(
                slope, partition, dims, refs, lambda g: got_cell(got, g), load, store,
                (0, share), sums, kept,
            )

        if share:
            pl.run_scoped(
                keep, *[pltpu.ACC(mxu_id=i % 2)(acc.shape, jnp.float32) for i in range(4)]
            )
        deposit_scope(*acc.shape, body)

    fill_table(table, plain, lambda c: melt[c])
    step(lambda g, f: got[pl.ds(g * (SEND * GROUP) + f, GROUP, stride=SEND), :], 0, None)
    for c in range(COMPS):
        fresh = diffused(melt[c], low_x[c], high_x[c], low_z[c], high_z[c], rate[c])
        melt_mid[c] = fresh + deposit_of(acc, c, size_x, size_y)
    fill_table(table, plain, lambda c: melt_mid[c])
    fill_lines(lines, lambda c: melt_mid[c], size_y)
    step(lambda g, f: back[stay(g, f), :], kept.shape[0], kept)


def kept_kernel(dims, got, kept, before, acc):

    def body(sums):
        def two(i, _):
            for g in (2 * i, 2 * i + 1):
                spend_group(got_cell(got, g), kept.at[g], dims, sums)
            return 0

        lax.fori_loop(0, kept.shape[0] // 2, two, 0)
        acc[...] = before[...] + (pltpu.matmul_pop(sums[0]) + pltpu.matmul_pop(sums[1]))

    deposit_scope(*acc.shape, body)


def finish_kernel(rate, melt, acc, low_x, high_x, low_z, high_z, out):
    size_y = low_x.shape[1]
    size_x = melt.shape[1] // size_y
    for c in range(COMPS):
        fresh = diffused(melt[c], low_x[c], high_x[c], low_z[c], high_z[c], rate[c])
        out[c] = fresh + deposit_of(acc, c, size_x, size_y)


def kernel_call(kernel, outs, in_specs, out_specs, scratch=(), limit=LIMIT, cost=None):
    return pl.pallas_call(
        kernel,
        out_shape=outs,
        in_specs=in_specs,
        out_specs=out_specs,
        scratch_shapes=list(scratch),
        compiler_params=pltpu.CompilerParams(vmem_limit_bytes=limit),
        cost_estimate=None
        if cost is None
        else pl.CostEstimate(flops=cost, bytes_accessed=2**20, transcendentals=0),
    )


def shape(*dims):
    return jax.ShapeDtypeStruct(dims, jnp.float32)


def neighbours(melt, size_y):
    def shift(edge, axis, step):
        n = lax.axis_size(axis)
        return lax.ppermute(edge, axis, [(i, i + step) for i in range(n) if 0 <= i + step < n])

    low_x = shift(melt[:, -size_y:, :], "brick", 1)
    high_x = shift(melt[:, :size_y, :], "brick", -1)
    low_z = shift(melt[:, :, -1], "sec", 1)[:, :, None]
    high_z = shift(melt[:, :, 0], "sec", -1)[:, :, None]
    return low_x, high_x, low_z, high_z


def run_steps(got, melt, halo, slope, partition, rate, size_y):
    comps, columns, size_z = melt.shape
    size_x = columns // size_y
    slots = got.shape[0] // SEND
    sums = shape(comps * size_y, size_x * size_z)
    return kernel_call(
        steps_kernel,
        (
            shape(slots * BACK, LANES),
            shape(comps, columns, size_z),
            sums,
            shape(slots // GROUP * 3 // 4, comps, GROUP, LANES),
        ),
        [SMEM, SMEM, SMEM] + [VMEM] * 6,
        (VMEM, VMEM, VMEM, VMEM),
        [
            pltpu.VMEM((PAIRS, columns, size_z), jnp.int32),
            pltpu.VMEM((columns, size_z), jnp.float32),
            pltpu.VMEM((comps * size_y, size_x * size_z), jnp.bfloat16),
            pltpu.VMEM((comps, GROUP, LANES), jnp.float32),
        ],
    )(slope, partition, rate, got, melt, *halo)


def run_kept(got, kept, before, dims):
    return kernel_call(
        functools.partial(kept_kernel, dims),
        shape(*before.shape),
        [VMEM] * 3,
        VMEM,
        cost=8_000_000_000,
    )(got, kept, before)


def exchange(rows, devices):
    each = rows.shape[0] // CAP
    swapped = lax.all_to_all(
        rows.reshape(each, CAP, LANES), AXES, split_axis=0, concat_axis=0, tiled=True
    )
    return swapped.reshape(rows.shape)


def local(melt, velocity, radius, cell, target, count, slope, partition, rate):
    devices = lax.axis_size(AXES)
    size_x, size_y, comps, size_z = melt.shape
    blocks = target.shape[0]
    slots = devices * CAP
    sent, slot_of = kernel_call(
        pack_kernel,
        (shape(slots * SEND, LANES), jax.ShapeDtypeStruct((blocks,), jnp.int32)),
        [HBM] * 5,
        (VMEM, SMEM),
        [
            pltpu.SMEM((blocks,), jnp.int32),
            pltpu.SMEM((blocks,), jnp.int32),
            pltpu.VMEM((3, blocks, LANES), jnp.float32),
            pltpu.VMEM((blocks, LANES), jnp.float32),
            pltpu.VMEM((blocks, LANES), jnp.int32),
            pltpu.SMEM((devices,), jnp.int32),
            pltpu.SemaphoreType.DMA((5,)),
        ],
        limit=WHOLE,
    )(target, count, jnp.transpose(velocity, (1, 0, 2)), radius, cell)
    got = exchange(sent, devices)
    start = jnp.transpose(melt, (2, 0, 1, 3)).reshape(comps, size_x * size_y, size_z)
    halo = neighbours(start, size_y)
    back, middle, acc, kept = run_steps(got, start, halo, slope, partition, rate, size_y)
    returned = exchange(back, devices)
    halo = neighbours(middle, size_y)
    acc = run_kept(got, kept, acc, (size_x, size_y, size_z))
    final = kernel_call(
        finish_kernel,
        shape(comps, size_x * size_y, size_z),
        [SMEM] + [VMEM] * 6,
        VMEM,
    )(rate, middle, acc, *halo)
    melt_out = jnp.transpose(final.reshape(comps, size_x, size_y, size_z), (1, 2, 0, 3))
    velocity_out, radius_out = kernel_call(
        unpack_kernel,
        (shape(3, blocks, LANES), shape(blocks, LANES)),
        [SMEM, VMEM],
        (HBM, HBM),
        [
            pltpu.VMEM((3, blocks, LANES), jnp.float32),
            pltpu.VMEM((blocks, LANES), jnp.float32),
            pltpu.SemaphoreType.DMA((4,)),
        ],
    )(slot_of, returned)
    return melt_out, jnp.transpose(velocity_out, (1, 0, 2)), radius_out


def solution(mesh):
    return jax.shard_map(
        local,
        mesh=mesh,
        in_specs=(
            P("brick", None, None, "sec"),
            P(AXES, None, None),
            P(AXES, None),
            P(AXES, None),
            P(AXES),
            P(AXES),
            P(),
            P(),
            P(),
        ),
        out_specs=(P("brick", None, None, "sec"), P(AXES, None, None), P(AXES, None)),
        check_vma=False,
    )
```

```python
import functools

import jax
import jax.numpy as jnp
from jax import lax
from jax.experimental import pallas as pl
from jax.experimental.pallas import tpu as pltpu
from jax.sharding import PartitionSpec as P

AXES = ("sec", "brick")
CAP = 4
LANES = 128
COMPS = 7
SEND = 5
BACK = 4
GROUP = 8
PAIRS = 3
TINY = 2.0**-126

GROW = 0.4
DRAG = 0.25
MOMENT = 0.4
LATENT = 0.5
SETTLE = 0.1

VMEM = pl.BlockSpec(memory_space=pltpu.VMEM)
SMEM = pl.BlockSpec(memory_space=pltpu.SMEM)
HBM = pl.BlockSpec(memory_space=pltpu.HBM)
LIMIT = 16 * 2**20
WHOLE = 64 * 2**20


def pack_kernel(
    target_hbm, count_hbm, velo_hbm, radi_hbm, cell_hbm,
    sent, slot_of, target, count, velo, radi, cell, seen, ready,
):
    blocks = radi.shape[0]
    bricks = seen.shape[0]
    pairs = [
        (target_hbm, target),
        (count_hbm, count),
        (velo_hbm, velo),
        (radi_hbm, radi),
        (cell_hbm, cell),
    ]
    copies = [
        pltpu.make_async_copy(source, into, ready.at[i]) for i, (source, into) in enumerate(pairs)
    ]
    for copy in copies:
        copy.start()

    def clear(i, _):
        seen[i] = 0
        return 0

    lax.fori_loop(0, bricks, clear, 0, unroll=16)
    sent[...] = jnp.full(sent.shape, -1.0, jnp.float32)
    lane = lax.broadcasted_iota(jnp.int32, (1, LANES), 1)
    copies[0].wait()

    def rank(k, _):
        brick = target[k]
        earlier = seen[brick]
        seen[brick] = earlier + 1
        slot_of[k] = brick * CAP + earlier
        return 0

    lax.fori_loop(0, blocks, rank, 0, unroll=16)
    for copy in copies[1:]:
        copy.wait()

    def place(k, _):
        row = slot_of[k] * SEND
        for c in range(3):
            sent[pl.ds(row + c, 1), :] = velo[c, pl.ds(k, 1), :]
        sent[pl.ds(row + 3, 1), :] = radi[pl.ds(k, 1), :]
        where = cell[pl.ds(k, 1), :].astype(jnp.float32)
        sent[pl.ds(row + 4, 1), :] = jnp.where(lane < count[k], where, -1.0)
        return 0

    lax.fori_loop(0, blocks, place, 0, unroll=8)


def unpack_kernel(slot_of, back, velo_hbm, radi_hbm, velo, radi, done):
    blocks = radi.shape[0]
    half = blocks // 2

    def place(k, _):
        row = slot_of[k] * BACK
        for c in range(3):
            velo[c, pl.ds(k, 1), :] = back[pl.ds(row + c, 1), :]
        radi[pl.ds(k, 1), :] = back[pl.ds(row + 3, 1), :]
        return 0

    copies = []
    for part in range(2):
        lax.fori_loop(part * half, (part + 1) * half, place, 0, unroll=8)
        own = pl.ds(part * half, half)
        copies += [
            pltpu.make_async_copy(velo.at[:, own], velo_hbm.at[:, own], done.at[2 * part]),
            pltpu.make_async_copy(radi.at[own], radi_hbm.at[own], done.at[2 * part + 1]),
        ]
        copies[-2].start()
        copies[-1].start()
    for copy in copies:
        copy.wait()


def diffused(melt, low_x, high_x, low_z, high_z, rate):
    rows, size_z = melt.shape
    size_y = low_x.shape[0]
    lane = lax.broadcasted_iota(jnp.int32, (rows, size_z), 1)
    level = lax.broadcasted_iota(jnp.int32, (rows, size_z), 0) % size_y
    below_x = jnp.concatenate([low_x, melt[:-size_y]], axis=0)
    above_x = jnp.concatenate([melt[size_y:], high_x], axis=0)
    below_y = jnp.where(level == 0, 0.0, pltpu.roll(melt, 1, 0))
    above_y = jnp.where(level == size_y - 1, 0.0, pltpu.roll(melt, rows - 1, 0))
    below_z = jnp.where(lane == 0, low_z, pltpu.roll(melt, 1, 1))
    above_z = jnp.where(lane == size_z - 1, high_z, pltpu.roll(melt, size_z - 1, 1))
    beside = above_x + below_x + above_y + below_y + above_z + below_z
    return melt + rate * (beside - 6.0 * melt)


def deposit_of(acc, comp, size_x, size_y):
    part = acc[comp * size_y : (comp + 1) * size_y, :]
    size_z = part.shape[1] // size_x
    return jnp.concatenate(
        [part[:, x * size_z : (x + 1) * size_z] for x in range(size_x)], axis=0
    )


def code_of(value):
    size = jnp.abs(value)
    exponent = jnp.floor(jnp.log2(jnp.maximum(size, TINY)))
    mantissa = size * power(-exponent)
    high = mantissa >= 2.0
    low = mantissa < 1.0
    exponent = jnp.where(high, exponent + 1.0, jnp.where(low, exponent - 1.0, exponent))
    mantissa = jnp.where(high, mantissa * 0.5, jnp.where(low, mantissa * 2.0, mantissa))
    code = (exponent + 126.0) * 128.0 + mantissa * 128.0
    code = jnp.where(size < TINY, 0.0, code)
    return jnp.where(value < 0.0, -code, code).astype(jnp.int32)


def value_of(code):
    size = jnp.abs(code)
    scale = power((size >> 7).astype(jnp.float32) - 127.0)
    value = ((size & 127) + 128).astype(jnp.float32) * (1.0 / 128.0) * scale
    value = jnp.where(size == 0, 0.0, value)
    return jnp.where(code < 0, -value, value)


def power(exponent):
    return jnp.exp2(exponent).astype(jnp.bfloat16).astype(jnp.float32)


def paired(high, low):
    return code_of(high) * 65536 + (code_of(low) & 65535)


def unpaired(found):
    first = [value_of(word >> 16) for word in found[:PAIRS]]
    second = [value_of((word << 16) >> 16) for word in found[:PAIRS]]
    return [*first, found[PAIRS], *second]


def spend_group(cell, fed_rows, dims, sums):
    size_x, size_y, size_z = dims
    row_iota = lax.broadcasted_iota(jnp.int32, (size_x * size_z, LANES), 0)
    y_iota = lax.broadcasted_iota(jnp.int32, (size_y, LANES), 0)
    z = cell & (size_z - 1)
    column = cell >> 7
    y = jnp.where(cell >= 0, column & (size_y - 1), size_y)
    line = ((column >> 4) * size_z) | z
    for t in range(GROUP // 2):
        lefts, rights = [], []
        for b in (2 * t, 2 * t + 1):
            mask = y_iota == y[b : b + 1, :]
            lefts.append(
                jnp.concatenate(
                    [
                        jnp.where(mask, fed_rows[c, b : b + 1, :], 0.0).astype(jnp.bfloat16)
                        for c in range(COMPS)
                    ],
                    axis=0,
                )
            )
            rights.append(
                jnp.where(row_iota == line[b : b + 1, :], 1.0, 0.0).astype(jnp.bfloat16)
            )
        unit, stage = t % 2, t // 2
        pltpu.matmul_push_rhs(
            jnp.concatenate(rights, axis=1),
            staging_register=stage,
            mxu_index=unit,
            transpose=True,
        )
        pltpu.matmul_acc_lhs(
            sums[unit], jnp.concatenate(lefts, axis=1), load_staged_rhs=stage
        )


def matrix_probe(cell, lines, dims, sums):
    size_x, size_y, size_z = dims
    row_iota = lax.broadcasted_iota(jnp.int32, (size_x * size_z, LANES), 0)
    y_iota = lax.broadcasted_iota(jnp.int32, (size_y, LANES), 0)
    column = cell >> 7
    y = jnp.where(cell >= 0, column & (size_y - 1), size_y)
    line = ((column >> 4) * size_z) | (cell & (size_z - 1))
    found = [[] for _ in range(COMPS)]
    for t in range(GROUP // 2):
        pair = (2 * t, 2 * t + 1)
        unit, stage = t % 2, t // 2
        pltpu.matmul_push_rhs(
            jnp.concatenate(
                [
                    jnp.where(row_iota == line[b : b + 1, :], 1.0, 0.0).astype(jnp.bfloat16)
                    for b in pair
                ],
                axis=1,
            ),
            staging_register=stage,
            mxu_index=unit,
        )
        pltpu.matmul_acc_lhs(sums[2 * stage + unit], lines[...], load_staged_rhs=stage)
        lifted = pltpu.matmul_pop(sums[2 * stage + unit])
        for i, b in enumerate(pair):
            mask = y_iota == y[b : b + 1, :]
            for c in range(COMPS):
                part = lifted[c * size_y : (c + 1) * size_y, i * LANES : (i + 1) * LANES]
                found[c].append(jnp.sum(jnp.where(mask, part, 0.0), axis=0, keepdims=True))
    return [jnp.concatenate(rows, axis=0) for rows in found]


def coupling_step(slope, partition, dims, refs, load_cell, load, store, span, sums, kept=None):
    size_x, size_y, size_z = dims
    table, plain, lines, fed_rows = refs
    columns = size_x * size_y

    def look(g):
        cell = load_cell(g)
        z = cell & (size_z - 1)
        column = cell >> 7
        words = [jnp.zeros((GROUP, LANES), jnp.int32)] * PAIRS
        single = jnp.zeros((GROUP, LANES), jnp.float32)
        for j in range(columns):
            here = column == j
            for c in range(PAIRS):
                row = jnp.broadcast_to(table[c, j : j + 1, :], (GROUP, LANES))
                words[c] = jnp.where(here, jnp.take_along_axis(row, z, axis=1), words[c])
            row = jnp.broadcast_to(plain[j : j + 1, :], (GROUP, LANES))
            single = jnp.where(here, jnp.take_along_axis(row, z, axis=1), single)
        return (*words, single)

    def work(g, probe, into):
        live = load_cell(g) >= 0
        velo = [load(g, 0), load(g, 1), load(g, 2)]
        radi = load(g, 3)
        under = (
            probe[4] * slope[0] + probe[5] * slope[1] + probe[6] * slope[2]
        ) - probe[3]
        growth = GROW * (jnp.maximum(under, 0.0) + jnp.log1p(jnp.exp(-jnp.abs(under))))
        beta = DRAG / (radi * radi)
        push = -(MOMENT * radi * radi * radi * beta)
        slip = [probe[c] - velo[c] for c in range(3)]
        fed = growth * radi
        sources = [push * slip[c] for c in range(3)] + [LATENT * growth * radi]
        sources += [(1.0 - partition[s]) * probe[4 + s] * fed for s in range(3)]
        new_velo = [velo[c] + beta * slip[c] for c in range(3)]
        new_velo[2] = new_velo[2] - SETTLE * radi
        new_radi = radi + growth / radi
        for c in range(3):
            store(g, c, jnp.where(live, new_velo[c], velo[c]))
        store(g, 3, jnp.where(live, new_radi, radi))
        for c in range(COMPS):
            into[c] = sources[c]
        if kept is not None:
            into[COMPS] = load_cell(g).astype(jnp.float32)

    def spend(g):
        spend_group(load_cell(g), fed_rows, dims, sums)

    first, stop = span
    last = stop - 1

    if kept is None:

        def group(g, found):
            spend(g - 1)
            later = look(jnp.minimum(g + 1, last))
            work(g, unpaired(found), fed_rows)
            return later

        def two(i, found):
            return group(2 * i + 1, group(2 * i, found))

        work(first, unpaired(look(first)), fed_rows)
        lax.fori_loop(first // 2 + 1, stop // 2, two, group(first + 1, look(first + 1)))
        spend(last)
    else:

        def pair(g):
            return look(g), tuple(matrix_probe(load_cell(g + 1), lines, dims, sums))

        def both(i, found):
            g = 2 * i
            later = pair(jnp.minimum(g + 2, last - 1))
            work(g, unpaired(found[0]), kept.at[g - first])
            work(g + 1, found[1], kept.at[g + 1 - first])
            return later

        def four(i, found):
            return both(2 * i + 1, both(2 * i, found))

        lax.fori_loop(first // 4, stop // 4, four, pair(first))


def deposit_scope(rows, width, body):
    pl.run_scoped(
        lambda *sums: body(sums),
        pltpu.ACC(mxu_id=0)((rows, width), jnp.float32),
        pltpu.ACC(mxu_id=1)((rows, width), jnp.float32),
    )


def fill_lines(lines, value, size_y):
    for c in range(COMPS):
        part = value(c).astype(jnp.bfloat16)
        lines[c * size_y : (c + 1) * size_y, :] = jnp.concatenate(
            [part[x : x + size_y] for x in range(0, part.shape[0], size_y)], axis=1
        )


def fill_table(table, plain, value):
    rounded = [value(c).astype(jnp.bfloat16).astype(jnp.float32) for c in range(COMPS)]
    for c in range(PAIRS):
        table[c] = paired(rounded[c], rounded[PAIRS + 1 + c])
    plain[...] = rounded[PAIRS]


def got_cell(got, g):
    return got[pl.ds(g * (SEND * GROUP) + 4, GROUP, stride=SEND), :].astype(jnp.int32)


def steps_kernel(
    slope, partition, rate, got, melt, low_x, high_x, low_z, high_z,
    back, melt_mid, acc, kept, *refs,
):
    table, plain, lines, _ = refs
    size_y = low_x.shape[1]
    size_x = melt.shape[1] // size_y
    dims = (size_x, size_y, melt.shape[2])
    groups = got.shape[0] // (SEND * GROUP)

    def stay(g, f):
        return pl.ds(g * (BACK * GROUP) + f, GROUP, stride=BACK)

    def store(g, f, value):
        back[stay(g, f), :] = value

    def step(load, share, kept):
        def body(sums):
            coupling_step(
                slope, partition, dims, refs, lambda g: got_cell(got, g), load, store,
                (share, groups), sums,
            )
            acc[...] = pltpu.matmul_pop(sums[0]) + pltpu.matmul_pop(sums[1])

        def keep(*sums):
            coupling_step(
                slope, partition, dims, refs, lambda g: got_cell(got, g), load, store,
                (0, share), sums, kept,
            )

        if share:
            pl.run_scoped(
                keep, *[pltpu.ACC(mxu_id=i % 2)(acc.shape, jnp.float32) for i in range(4)]
            )
        deposit_scope(*acc.shape, body)

    fill_table(table, plain, lambda c: melt[c])
    step(lambda g, f: got[pl.ds(g * (SEND * GROUP) + f, GROUP, stride=SEND), :], 0, None)
    for c in range(COMPS):
        fresh = diffused(melt[c], low_x[c], high_x[c], low_z[c], high_z[c], rate[c])
        melt_mid[c] = fresh + deposit_of(acc, c, size_x, size_y)
    fill_table(table, plain, lambda c: melt_mid[c])
    fill_lines(lines, lambda c: melt_mid[c], size_y)
    step(lambda g, f: back[stay(g, f), :], kept.shape[0], kept)


def kept_kernel(dims, kept, before, acc):

    def body(sums):
        def two(i, _):
            for g in (2 * i, 2 * i + 1):
                spend_group(kept[g, COMPS].astype(jnp.int32), kept.at[g], dims, sums)
            return 0

        lax.fori_loop(0, kept.shape[0] // 2, two, 0)
        acc[...] = before[...] + (pltpu.matmul_pop(sums[0]) + pltpu.matmul_pop(sums[1]))

    deposit_scope(*acc.shape, body)


def finish_kernel(rate, melt, acc, low_x, high_x, low_z, high_z, out):
    size_y = low_x.shape[1]
    size_x = melt.shape[1] // size_y
    for c in range(COMPS):
        fresh = diffused(melt[c], low_x[c], high_x[c], low_z[c], high_z[c], rate[c])
        out[c] = fresh + deposit_of(acc, c, size_x, size_y)


def kernel_call(kernel, outs, in_specs, out_specs, scratch=(), limit=LIMIT, cost=None):
    return pl.pallas_call(
        kernel,
        out_shape=outs,
        in_specs=in_specs,
        out_specs=out_specs,
        scratch_shapes=list(scratch),
        compiler_params=pltpu.CompilerParams(vmem_limit_bytes=limit),
        cost_estimate=None
        if cost is None
        else pl.CostEstimate(flops=cost, bytes_accessed=2**20, transcendentals=0),
    )


def shape(*dims):
    return jax.ShapeDtypeStruct(dims, jnp.float32)


def neighbours(melt, size_y):
    def shift(edge, axis, step):
        n = lax.axis_size(axis)
        return lax.ppermute(edge, axis, [(i, i + step) for i in range(n) if 0 <= i + step < n])

    low_x = shift(melt[:, -size_y:, :], "brick", 1)
    high_x = shift(melt[:, :size_y, :], "brick", -1)
    low_z = shift(melt[:, :, -1], "sec", 1)[:, :, None]
    high_z = shift(melt[:, :, 0], "sec", -1)[:, :, None]
    return low_x, high_x, low_z, high_z


def run_steps(got, melt, halo, slope, partition, rate, size_y):
    comps, columns, size_z = melt.shape
    size_x = columns // size_y
    slots = got.shape[0] // SEND
    sums = shape(comps * size_y, size_x * size_z)
    return kernel_call(
        steps_kernel,
        (
            shape(slots * BACK, LANES),
            shape(comps, columns, size_z),
            sums,
            shape(slots // GROUP * 5 // 8, comps + 1, GROUP, LANES),
        ),
        [SMEM, SMEM, SMEM] + [VMEM] * 6,
        (VMEM, VMEM, VMEM, VMEM),
        [
            pltpu.VMEM((PAIRS, columns, size_z), jnp.int32),
            pltpu.VMEM((columns, size_z), jnp.float32),
            pltpu.VMEM((comps * size_y, size_x * size_z), jnp.bfloat16),
            pltpu.VMEM((comps, GROUP, LANES), jnp.float32),
        ],
    )(slope, partition, rate, got, melt, *halo)


def run_kept(kept, before, dims):
    return kernel_call(
        functools.partial(kept_kernel, dims),
        shape(*before.shape),
        [VMEM] * 2,
        VMEM,
        cost=8_000_000_000,
    )(kept, before)


def exchange(rows, devices):
    each = rows.shape[0] // CAP
    swapped = lax.all_to_all(
        rows.reshape(each, CAP, LANES), AXES, split_axis=0, concat_axis=0, tiled=True
    )
    return swapped.reshape(rows.shape)


def local(melt, velocity, radius, cell, target, count, slope, partition, rate):
    devices = lax.axis_size(AXES)
    size_x, size_y, comps, size_z = melt.shape
    blocks = target.shape[0]
    slots = devices * CAP
    sent, slot_of = kernel_call(
        pack_kernel,
        (shape(slots * SEND, LANES), jax.ShapeDtypeStruct((blocks,), jnp.int32)),
        [HBM] * 5,
        (VMEM, SMEM),
        [
            pltpu.SMEM((blocks,), jnp.int32),
            pltpu.SMEM((blocks,), jnp.int32),
            pltpu.VMEM((3, blocks, LANES), jnp.float32),
            pltpu.VMEM((blocks, LANES), jnp.float32),
            pltpu.VMEM((blocks, LANES), jnp.int32),
            pltpu.SMEM((devices,), jnp.int32),
            pltpu.SemaphoreType.DMA((5,)),
        ],
        limit=WHOLE,
    )(target, count, jnp.transpose(velocity, (1, 0, 2)), radius, cell)
    got = exchange(sent, devices)
    start = jnp.transpose(melt, (2, 0, 1, 3)).reshape(comps, size_x * size_y, size_z)
    halo = neighbours(start, size_y)
    back, middle, acc, kept = run_steps(got, start, halo, slope, partition, rate, size_y)
    returned = exchange(back, devices)
    halo = neighbours(middle, size_y)
    acc = run_kept(kept, acc, (size_x, size_y, size_z))
    final = kernel_call(
        finish_kernel,
        shape(comps, size_x * size_y, size_z),
        [SMEM] + [VMEM] * 6,
        VMEM,
    )(rate, middle, acc, *halo)
    melt_out = jnp.transpose(final.reshape(comps, size_x, size_y, size_z), (1, 2, 0, 3))
    velocity_out, radius_out = kernel_call(
        unpack_kernel,
        (shape(3, blocks, LANES), shape(blocks, LANES)),
        [SMEM, VMEM],
        (HBM, HBM),
        [
            pltpu.VMEM((3, blocks, LANES), jnp.float32),
            pltpu.VMEM((blocks, LANES), jnp.float32),
            pltpu.SemaphoreType.DMA((4,)),
        ],
    )(slot_of, returned)
    return melt_out, jnp.transpose(velocity_out, (1, 0, 2)), radius_out


def solution(mesh):
    return jax.shard_map(
        local,
        mesh=mesh,
        in_specs=(
            P("brick", None, None, "sec"),
            P(AXES, None, None),
            P(AXES, None),
            P(AXES, None),
            P(AXES),
            P(AXES),
            P(),
            P(),
            P(),
        ),
        out_specs=(P("brick", None, None, "sec"), P(AXES, None, None), P(AXES, None)),
        check_vma=False,
    )
```

```python
import functools

import jax
import jax.numpy as jnp
from jax import lax
from jax.experimental import pallas as pl
from jax.experimental.pallas import tpu as pltpu
from jax.sharding import PartitionSpec as P

AXES = ("sec", "brick")
CAP = 4
LANES = 128
COMPS = 7
SEND = 5
BACK = 4
GROUP = 8
PAIRS = 3
TINY = 2.0**-126

GROW = 0.4
DRAG = 0.25
MOMENT = 0.4
LATENT = 0.5
SETTLE = 0.1

VMEM = pl.BlockSpec(memory_space=pltpu.VMEM)
SMEM = pl.BlockSpec(memory_space=pltpu.SMEM)
HBM = pl.BlockSpec(memory_space=pltpu.HBM)
LIMIT = 16 * 2**20
WHOLE = 64 * 2**20


def pack_kernel(
    target_hbm, count_hbm, velo_hbm, radi_hbm, cell_hbm,
    sent, slot_of, target, count, velo, radi, cell, seen, ready,
):
    blocks = radi.shape[0]
    bricks = seen.shape[0]
    pairs = [
        (target_hbm, target),
        (count_hbm, count),
        (velo_hbm, velo),
        (radi_hbm, radi),
        (cell_hbm, cell),
    ]
    copies = [
        pltpu.make_async_copy(source, into, ready.at[i]) for i, (source, into) in enumerate(pairs)
    ]
    for copy in copies:
        copy.start()

    def clear(i, _):
        seen[i] = 0
        return 0

    lax.fori_loop(0, bricks, clear, 0, unroll=16)
    sent[...] = jnp.full(sent.shape, -1.0, jnp.float32)
    lane = lax.broadcasted_iota(jnp.int32, (1, LANES), 1)
    copies[0].wait()

    def rank(k, _):
        brick = target[k]
        earlier = seen[brick]
        seen[brick] = earlier + 1
        slot_of[k] = brick * CAP + earlier
        return 0

    lax.fori_loop(0, blocks, rank, 0, unroll=16)
    for copy in copies[1:]:
        copy.wait()

    def place(k, _):
        row = slot_of[k] * SEND
        for c in range(3):
            sent[pl.ds(row + c, 1), :] = velo[c, pl.ds(k, 1), :]
        sent[pl.ds(row + 3, 1), :] = radi[pl.ds(k, 1), :]
        where = cell[pl.ds(k, 1), :].astype(jnp.float32)
        sent[pl.ds(row + 4, 1), :] = jnp.where(lane < count[k], where, -1.0)
        return 0

    lax.fori_loop(0, blocks, place, 0, unroll=8)


def unpack_kernel(slot_of, back, velo_hbm, radi_hbm, velo, radi, done):
    blocks = radi.shape[0]
    half = blocks // 2

    def place(k, _):
        row = slot_of[k] * BACK
        for c in range(3):
            velo[c, pl.ds(k, 1), :] = back[pl.ds(row + c, 1), :]
        radi[pl.ds(k, 1), :] = back[pl.ds(row + 3, 1), :]
        return 0

    copies = []
    for part in range(2):
        lax.fori_loop(part * half, (part + 1) * half, place, 0, unroll=8)
        own = pl.ds(part * half, half)
        copies += [
            pltpu.make_async_copy(velo.at[:, own], velo_hbm.at[:, own], done.at[2 * part]),
            pltpu.make_async_copy(radi.at[own], radi_hbm.at[own], done.at[2 * part + 1]),
        ]
        copies[-2].start()
        copies[-1].start()
    for copy in copies:
        copy.wait()


def diffused(melt, low_x, high_x, low_z, high_z, rate):
    rows, size_z = melt.shape
    size_y = low_x.shape[0]
    lane = lax.broadcasted_iota(jnp.int32, (rows, size_z), 1)
    level = lax.broadcasted_iota(jnp.int32, (rows, size_z), 0) % size_y
    below_x = jnp.concatenate([low_x, melt[:-size_y]], axis=0)
    above_x = jnp.concatenate([melt[size_y:], high_x], axis=0)
    below_y = jnp.where(level == 0, 0.0, pltpu.roll(melt, 1, 0))
    above_y = jnp.where(level == size_y - 1, 0.0, pltpu.roll(melt, rows - 1, 0))
    below_z = jnp.where(lane == 0, low_z, pltpu.roll(melt, 1, 1))
    above_z = jnp.where(lane == size_z - 1, high_z, pltpu.roll(melt, size_z - 1, 1))
    beside = above_x + below_x + above_y + below_y + above_z + below_z
    return melt + rate * (beside - 6.0 * melt)


def deposit_of(acc, comp, size_x, size_y):
    part = acc[comp * size_y : (comp + 1) * size_y, :]
    size_z = part.shape[1] // size_x
    return jnp.concatenate(
        [part[:, x * size_z : (x + 1) * size_z] for x in range(size_x)], axis=0
    )


def code_of(value):
    size = jnp.abs(value)
    exponent = jnp.floor(jnp.log2(jnp.maximum(size, TINY)))
    mantissa = size * power(-exponent)
    high = mantissa >= 2.0
    low = mantissa < 1.0
    exponent = jnp.where(high, exponent + 1.0, jnp.where(low, exponent - 1.0, exponent))
    mantissa = jnp.where(high, mantissa * 0.5, jnp.where(low, mantissa * 2.0, mantissa))
    code = (exponent + 126.0) * 128.0 + mantissa * 128.0
    code = jnp.where(size < TINY, 0.0, code)
    return jnp.where(value < 0.0, -code, code).astype(jnp.int32)


def value_of(code):
    size = jnp.abs(code)
    scale = power((size >> 7).astype(jnp.float32) - 127.0)
    value = ((size & 127) + 128).astype(jnp.float32) * (1.0 / 128.0) * scale
    value = jnp.where(size == 0, 0.0, value)
    return jnp.where(code < 0, -value, value)


def power(exponent):
    return jnp.exp2(exponent).astype(jnp.bfloat16).astype(jnp.float32)


def paired(high, low):
    return code_of(high) * 65536 + (code_of(low) & 65535)


def unpaired(found):
    first = [value_of(word >> 16) for word in found[:PAIRS]]
    second = [value_of((word << 16) >> 16) for word in found[:PAIRS]]
    return [*first, found[PAIRS], *second]


def spend_group(cell, fed_rows, dims, sums):
    size_x, size_y, size_z = dims
    row_iota = lax.broadcasted_iota(jnp.int32, (size_x * size_z, LANES), 0)
    y_iota = lax.broadcasted_iota(jnp.int32, (size_y, LANES), 0)
    z = cell & (size_z - 1)
    column = cell >> 7
    y = jnp.where(cell >= 0, column & (size_y - 1), size_y)
    line = ((column >> 4) * size_z) | z
    for t in range(GROUP // 2):
        lefts, rights = [], []
        for b in (2 * t, 2 * t + 1):
            mask = y_iota == y[b : b + 1, :]
            lefts.append(
                jnp.concatenate(
                    [
                        jnp.where(mask, fed_rows[c, b : b + 1, :], 0.0).astype(jnp.bfloat16)
                        for c in range(COMPS)
                    ],
                    axis=0,
                )
            )
            rights.append(
                jnp.where(row_iota == line[b : b + 1, :], 1.0, 0.0).astype(jnp.bfloat16)
            )
        unit, stage = t % 2, t // 2
        pltpu.matmul_push_rhs(
            jnp.concatenate(rights, axis=1),
            staging_register=stage,
            mxu_index=unit,
            transpose=True,
        )
        pltpu.matmul_acc_lhs(
            sums[unit], jnp.concatenate(lefts, axis=1), load_staged_rhs=stage
        )


def matrix_probe(cell, lines, dims, sums):
    size_x, size_y, size_z = dims
    row_iota = lax.broadcasted_iota(jnp.int32, (size_x * size_z, LANES), 0)
    y_iota = lax.broadcasted_iota(jnp.int32, (size_y, LANES), 0)
    column = cell >> 7
    y = jnp.where(cell >= 0, column & (size_y - 1), size_y)
    line = ((column >> 4) * size_z) | (cell & (size_z - 1))
    found = [[] for _ in range(COMPS)]
    for t in range(GROUP // 2):
        pair = (2 * t, 2 * t + 1)
        unit, stage = t % 2, t // 2
        pltpu.matmul_push_rhs(
            jnp.concatenate(
                [
                    jnp.where(row_iota == line[b : b + 1, :], 1.0, 0.0).astype(jnp.bfloat16)
                    for b in pair
                ],
                axis=1,
            ),
            staging_register=stage,
            mxu_index=unit,
        )
        pltpu.matmul_acc_lhs(sums[2 * stage + unit], lines[...], load_staged_rhs=stage)
        lifted = pltpu.matmul_pop(sums[2 * stage + unit])
        for i, b in enumerate(pair):
            mask = y_iota == y[b : b + 1, :]
            for c in range(COMPS):
                part = lifted[c * size_y : (c + 1) * size_y, i * LANES : (i + 1) * LANES]
                found[c].append(jnp.sum(jnp.where(mask, part, 0.0), axis=0, keepdims=True))
    return [jnp.concatenate(rows, axis=0) for rows in found]


def coupling_step(slope, partition, dims, refs, load_cell, load, store, span, sums, kept=None):
    size_x, size_y, size_z = dims
    table, plain, lines, fed_rows = refs
    columns = size_x * size_y

    def look(g):
        cell = load_cell(g)
        z = cell & (size_z - 1)
        column = cell >> 7
        words = [jnp.zeros((GROUP, LANES), jnp.int32)] * PAIRS
        single = jnp.zeros((GROUP, LANES), jnp.float32)
        for j in range(columns):
            here = column == j
            for c in range(PAIRS):
                row = jnp.broadcast_to(table[c, j : j + 1, :], (GROUP, LANES))
                words[c] = jnp.where(here, jnp.take_along_axis(row, z, axis=1), words[c])
            row = jnp.broadcast_to(plain[j : j + 1, :], (GROUP, LANES))
            single = jnp.where(here, jnp.take_along_axis(row, z, axis=1), single)
        return (*words, single)

    def work(g, probe, into):
        live = load_cell(g) >= 0
        velo = [load(g, 0), load(g, 1), load(g, 2)]
        radi = load(g, 3)
        under = (
            probe[4] * slope[0] + probe[5] * slope[1] + probe[6] * slope[2]
        ) - probe[3]
        growth = GROW * (jnp.maximum(under, 0.0) + jnp.log1p(jnp.exp(-jnp.abs(under))))
        beta = DRAG / (radi * radi)
        push = -(MOMENT * radi * radi * radi * beta)
        slip = [probe[c] - velo[c] for c in range(3)]
        fed = growth * radi
        sources = [push * slip[c] for c in range(3)] + [LATENT * growth * radi]
        sources += [(1.0 - partition[s]) * probe[4 + s] * fed for s in range(3)]
        new_velo = [velo[c] + beta * slip[c] for c in range(3)]
        new_velo[2] = new_velo[2] - SETTLE * radi
        new_radi = radi + growth / radi
        for c in range(3):
            store(g, c, jnp.where(live, new_velo[c], velo[c]))
        store(g, 3, jnp.where(live, new_radi, radi))
        for c in range(COMPS):
            into[c] = sources[c]
        if kept is not None:
            into[COMPS] = load_cell(g).astype(jnp.float32)

    def spend(g):
        spend_group(load_cell(g), fed_rows, dims, sums)

    first, stop = span
    last = stop - 1

    if kept is None:

        def group(g, found):
            spend(g - 1)
            later = look(jnp.minimum(g + 1, last))
            work(g, unpaired(found), fed_rows)
            return later

        def four(i, found):
            for r in range(4):
                found = group(4 * i + r, found)
            return found

        work(first, unpaired(look(first)), fed_rows)
        found = look(first + 1)
        for r in range(1, 4):
            found = group(first + r, found)
        lax.fori_loop(first // 4 + 1, stop // 4, four, found)
        spend(last)
    else:

        def pair(g):
            return look(g), tuple(matrix_probe(load_cell(g + 1), lines, dims, sums))

        def both(i, found):
            g = 2 * i
            later = pair(jnp.minimum(g + 2, last - 1))
            work(g, unpaired(found[0]), kept.at[g - first])
            work(g + 1, found[1], kept.at[g + 1 - first])
            return later

        def four(i, found):
            return both(2 * i + 1, both(2 * i, found))

        lax.fori_loop(first // 4, stop // 4, four, pair(first))


def deposit_scope(rows, width, body):
    pl.run_scoped(
        lambda *sums: body(sums),
        pltpu.ACC(mxu_id=0)((rows, width), jnp.float32),
        pltpu.ACC(mxu_id=1)((rows, width), jnp.float32),
    )


def fill_lines(lines, value, size_y):
    for c in range(COMPS):
        part = value(c).astype(jnp.bfloat16)
        lines[c * size_y : (c + 1) * size_y, :] = jnp.concatenate(
            [part[x : x + size_y] for x in range(0, part.shape[0], size_y)], axis=1
        )


def fill_table(table, plain, value):
    rounded = [value(c).astype(jnp.bfloat16).astype(jnp.float32) for c in range(COMPS)]
    for c in range(PAIRS):
        table[c] = paired(rounded[c], rounded[PAIRS + 1 + c])
    plain[...] = rounded[PAIRS]


def got_cell(got, g):
    return got[pl.ds(g * (SEND * GROUP) + 4, GROUP, stride=SEND), :].astype(jnp.int32)


def steps_kernel(
    slope, partition, rate, got, melt, low_x, high_x, low_z, high_z,
    back, melt_mid, acc, kept, *refs,
):
    table, plain, lines, _ = refs
    size_y = low_x.shape[1]
    size_x = melt.shape[1] // size_y
    dims = (size_x, size_y, melt.shape[2])
    groups = got.shape[0] // (SEND * GROUP)

    def stay(g, f):
        return pl.ds(g * (BACK * GROUP) + f, GROUP, stride=BACK)

    def store(g, f, value):
        back[stay(g, f), :] = value

    def step(load, share, kept):
        def body(sums):
            coupling_step(
                slope, partition, dims, refs, lambda g: got_cell(got, g), load, store,
                (share, groups), sums,
            )
            acc[...] = pltpu.matmul_pop(sums[0]) + pltpu.matmul_pop(sums[1])

        def keep(*sums):
            coupling_step(
                slope, partition, dims, refs, lambda g: got_cell(got, g), load, store,
                (0, share), sums, kept,
            )

        if share:
            pl.run_scoped(
                keep, *[pltpu.ACC(mxu_id=i % 2)(acc.shape, jnp.float32) for i in range(4)]
            )
        deposit_scope(*acc.shape, body)

    fill_table(table, plain, lambda c: melt[c])
    step(lambda g, f: got[pl.ds(g * (SEND * GROUP) + f, GROUP, stride=SEND), :], 0, None)
    for c in range(COMPS):
        fresh = diffused(melt[c], low_x[c], high_x[c], low_z[c], high_z[c], rate[c])
        melt_mid[c] = fresh + deposit_of(acc, c, size_x, size_y)
    fill_table(table, plain, lambda c: melt_mid[c])
    fill_lines(lines, lambda c: melt_mid[c], size_y)
    step(lambda g, f: back[stay(g, f), :], kept.shape[0], kept)


def kept_kernel(dims, kept, before, acc):

    def body(sums):
        def two(i, _):
            for g in (2 * i, 2 * i + 1):
                spend_group(kept[g, COMPS].astype(jnp.int32), kept.at[g], dims, sums)
            return 0

        lax.fori_loop(0, kept.shape[0] // 2, two, 0)
        acc[...] = before[...] + (pltpu.matmul_pop(sums[0]) + pltpu.matmul_pop(sums[1]))

    deposit_scope(*acc.shape, body)


def finish_kernel(rate, melt, acc, low_x, high_x, low_z, high_z, out):
    size_y = low_x.shape[1]
    size_x = melt.shape[1] // size_y
    for c in range(COMPS):
        fresh = diffused(melt[c], low_x[c], high_x[c], low_z[c], high_z[c], rate[c])
        fresh = fresh + deposit_of(acc, c, size_x, size_y)
        for x in range(size_x):
            out[x, c] = fresh[x * size_y : (x + 1) * size_y]


def kernel_call(kernel, outs, in_specs, out_specs, scratch=(), limit=LIMIT, cost=None):
    return pl.pallas_call(
        kernel,
        out_shape=outs,
        in_specs=in_specs,
        out_specs=out_specs,
        scratch_shapes=list(scratch),
        compiler_params=pltpu.CompilerParams(vmem_limit_bytes=limit),
        cost_estimate=None
        if cost is None
        else pl.CostEstimate(flops=cost, bytes_accessed=2**20, transcendentals=0),
    )


def shape(*dims):
    return jax.ShapeDtypeStruct(dims, jnp.float32)


def neighbours(melt, size_y):
    def shift(edge, axis, step):
        n = lax.axis_size(axis)
        return lax.ppermute(edge, axis, [(i, i + step) for i in range(n) if 0 <= i + step < n])

    low_x = shift(melt[:, -size_y:, :], "brick", 1)
    high_x = shift(melt[:, :size_y, :], "brick", -1)
    low_z = shift(melt[:, :, -1], "sec", 1)[:, :, None]
    high_z = shift(melt[:, :, 0], "sec", -1)[:, :, None]
    return low_x, high_x, low_z, high_z


def run_steps(got, melt, halo, slope, partition, rate, size_y):
    comps, columns, size_z = melt.shape
    size_x = columns // size_y
    slots = got.shape[0] // SEND
    sums = shape(comps * size_y, size_x * size_z)
    return kernel_call(
        steps_kernel,
        (
            shape(slots * BACK, LANES),
            shape(comps, columns, size_z),
            sums,
            shape(slots // GROUP // 2, comps + 1, GROUP, LANES),
        ),
        [SMEM, SMEM, SMEM] + [VMEM] * 6,
        (VMEM, VMEM, VMEM, VMEM),
        [
            pltpu.VMEM((PAIRS, columns, size_z), jnp.int32),
            pltpu.VMEM((columns, size_z), jnp.float32),
            pltpu.VMEM((comps * size_y, size_x * size_z), jnp.bfloat16),
            pltpu.VMEM((comps, GROUP, LANES), jnp.float32),
        ],
    )(slope, partition, rate, got, melt, *halo)


def run_kept(kept, before, dims):
    return kernel_call(
        functools.partial(kept_kernel, dims),
        shape(*before.shape),
        [VMEM] * 2,
        VMEM,
        cost=8_000_000_000,
    )(kept, before)


def exchange(rows, devices):
    each = rows.shape[0] // CAP
    swapped = lax.all_to_all(
        rows.reshape(each, CAP, LANES), AXES, split_axis=0, concat_axis=0, tiled=True
    )
    return swapped.reshape(rows.shape)


def local(melt, velocity, radius, cell, target, count, slope, partition, rate):
    devices = lax.axis_size(AXES)
    size_x, size_y, comps, size_z = melt.shape
    blocks = target.shape[0]
    slots = devices * CAP
    sent, slot_of = kernel_call(
        pack_kernel,
        (shape(slots * SEND, LANES), jax.ShapeDtypeStruct((blocks,), jnp.int32)),
        [HBM] * 5,
        (VMEM, SMEM),
        [
            pltpu.SMEM((blocks,), jnp.int32),
            pltpu.SMEM((blocks,), jnp.int32),
            pltpu.VMEM((3, blocks, LANES), jnp.float32),
            pltpu.VMEM((blocks, LANES), jnp.float32),
            pltpu.VMEM((blocks, LANES), jnp.int32),
            pltpu.SMEM((devices,), jnp.int32),
            pltpu.SemaphoreType.DMA((5,)),
        ],
        limit=WHOLE,
    )(target, count, jnp.transpose(velocity, (1, 0, 2)), radius, cell)
    got = exchange(sent, devices)
    start = jnp.transpose(melt, (2, 0, 1, 3)).reshape(comps, size_x * size_y, size_z)
    halo = neighbours(start, size_y)
    back, middle, acc, kept = run_steps(got, start, halo, slope, partition, rate, size_y)
    returned = exchange(back, devices)
    halo = neighbours(middle, size_y)
    acc = run_kept(kept, acc, (size_x, size_y, size_z))
    final = kernel_call(
        finish_kernel,
        shape(size_x, comps, size_y, size_z),
        [SMEM] + [VMEM] * 6,
        VMEM,
    )(rate, middle, acc, *halo)
    melt_out = jnp.transpose(final, (0, 2, 1, 3))
    velocity_out, radius_out = kernel_call(
        unpack_kernel,
        (shape(3, blocks, LANES), shape(blocks, LANES)),
        [SMEM, VMEM],
        (HBM, HBM),
        [
            pltpu.VMEM((3, blocks, LANES), jnp.float32),
            pltpu.VMEM((blocks, LANES), jnp.float32),
            pltpu.SemaphoreType.DMA((4,)),
        ],
    )(slot_of, returned)
    return melt_out, jnp.transpose(velocity_out, (1, 0, 2)), radius_out


def solution(mesh):
    return jax.shard_map(
        local,
        mesh=mesh,
        in_specs=(
            P("brick", None, None, "sec"),
            P(AXES, None, None),
            P(AXES, None),
            P(AXES, None),
            P(AXES),
            P(AXES),
            P(),
            P(),
            P(),
        ),
        out_specs=(P("brick", None, None, "sec"), P(AXES, None, None), P(AXES, None)),
        check_vma=False,
    )
```

```python
import functools

import jax
import jax.numpy as jnp
from jax import lax
from jax.experimental import pallas as pl
from jax.experimental.pallas import tpu as pltpu
from jax.sharding import PartitionSpec as P

AXES = ("sec", "brick")
CAP = 4
LANES = 128
COMPS = 7
SEND = 5
BACK = 4
GROUP = 8
PAIRS = 3
TINY = 2.0**-126

GROW = 0.4
DRAG = 0.25
MOMENT = 0.4
LATENT = 0.5
SETTLE = 0.1

VMEM = pl.BlockSpec(memory_space=pltpu.VMEM)
SMEM = pl.BlockSpec(memory_space=pltpu.SMEM)
HBM = pl.BlockSpec(memory_space=pltpu.HBM)
LIMIT = 16 * 2**20
WHOLE = 64 * 2**20


def pack_kernel(
    target_hbm, count_hbm, velo_hbm, radi_hbm, cell_hbm,
    sent, slot_of, target, count, velo, radi, cell, seen, ready,
):
    blocks = radi.shape[0]
    bricks = seen.shape[0]
    pairs = [
        (target_hbm, target),
        (count_hbm, count),
        (velo_hbm, velo),
        (radi_hbm, radi),
        (cell_hbm, cell),
    ]
    copies = [
        pltpu.make_async_copy(source, into, ready.at[i]) for i, (source, into) in enumerate(pairs)
    ]
    for copy in copies:
        copy.start()

    def clear(i, _):
        seen[i] = 0
        return 0

    lax.fori_loop(0, bricks, clear, 0, unroll=16)
    sent[...] = jnp.full(sent.shape, -1.0, jnp.float32)
    lane = lax.broadcasted_iota(jnp.int32, (1, LANES), 1)
    copies[0].wait()

    def rank(k, _):
        brick = target[k]
        earlier = seen[brick]
        seen[brick] = earlier + 1
        slot_of[k] = brick * CAP + earlier
        return 0

    lax.fori_loop(0, blocks, rank, 0, unroll=16)
    for copy in copies[1:]:
        copy.wait()

    def place(k, _):
        row = slot_of[k] * SEND
        for c in range(3):
            sent[pl.ds(row + c, 1), :] = velo[c, pl.ds(k, 1), :]
        sent[pl.ds(row + 3, 1), :] = radi[pl.ds(k, 1), :]
        where = cell[pl.ds(k, 1), :].astype(jnp.float32)
        sent[pl.ds(row + 4, 1), :] = jnp.where(lane < count[k], where, -1.0)
        return 0

    lax.fori_loop(0, blocks, place, 0, unroll=8)


def unpack_kernel(slot_of, back, velo_hbm, radi_hbm, velo, radi, done):
    blocks = radi.shape[0]
    half = blocks // 2

    def place(k, _):
        row = slot_of[k] * BACK
        for c in range(3):
            velo[c, pl.ds(k, 1), :] = back[pl.ds(row + c, 1), :]
        radi[pl.ds(k, 1), :] = back[pl.ds(row + 3, 1), :]
        return 0

    copies = []
    for part in range(2):
        lax.fori_loop(part * half, (part + 1) * half, place, 0, unroll=8)
        own = pl.ds(part * half, half)
        copies += [
            pltpu.make_async_copy(velo.at[:, own], velo_hbm.at[:, own], done.at[2 * part]),
            pltpu.make_async_copy(radi.at[own], radi_hbm.at[own], done.at[2 * part + 1]),
        ]
        copies[-2].start()
        copies[-1].start()
    for copy in copies:
        copy.wait()


def diffused(melt, low_x, high_x, low_z, high_z, rate):
    rows, size_z = melt.shape
    size_y = low_x.shape[0]
    lane = lax.broadcasted_iota(jnp.int32, (rows, size_z), 1)
    level = lax.broadcasted_iota(jnp.int32, (rows, size_z), 0) % size_y
    below_x = jnp.concatenate([low_x, melt[:-size_y]], axis=0)
    above_x = jnp.concatenate([melt[size_y:], high_x], axis=0)
    below_y = jnp.where(level == 0, 0.0, pltpu.roll(melt, 1, 0))
    above_y = jnp.where(level == size_y - 1, 0.0, pltpu.roll(melt, rows - 1, 0))
    below_z = jnp.where(lane == 0, low_z, pltpu.roll(melt, 1, 1))
    above_z = jnp.where(lane == size_z - 1, high_z, pltpu.roll(melt, size_z - 1, 1))
    beside = above_x + below_x + above_y + below_y + above_z + below_z
    return melt + rate * (beside - 6.0 * melt)


def deposit_of(acc, comp, size_x, size_y):
    part = acc[comp * size_y : (comp + 1) * size_y, :]
    size_z = part.shape[1] // size_x
    return jnp.concatenate(
        [part[:, x * size_z : (x + 1) * size_z] for x in range(size_x)], axis=0
    )


def code_of(value):
    size = jnp.abs(value)
    exponent = jnp.floor(jnp.log2(jnp.maximum(size, TINY)))
    mantissa = size * power(-exponent)
    high = mantissa >= 2.0
    low = mantissa < 1.0
    exponent = jnp.where(high, exponent + 1.0, jnp.where(low, exponent - 1.0, exponent))
    mantissa = jnp.where(high, mantissa * 0.5, jnp.where(low, mantissa * 2.0, mantissa))
    code = (exponent + 126.0) * 128.0 + mantissa * 128.0
    code = jnp.where(size < TINY, 0.0, code)
    return jnp.where(value < 0.0, -code, code).astype(jnp.int32)


def value_of(code):
    size = jnp.abs(code)
    scale = power((size >> 7).astype(jnp.float32) - 127.0)
    value = ((size & 127) + 128).astype(jnp.float32) * (1.0 / 128.0) * scale
    value = jnp.where(size == 0, 0.0, value)
    return jnp.where(code < 0, -value, value)


def power(exponent):
    return jnp.exp2(exponent).astype(jnp.bfloat16).astype(jnp.float32)


def paired(high, low):
    return code_of(high) * 65536 + (code_of(low) & 65535)


def unpaired(found):
    first = [value_of(word >> 16) for word in found[:PAIRS]]
    second = [value_of((word << 16) >> 16) for word in found[:PAIRS]]
    return [*first, found[PAIRS], *second]


def spend_group(cell, fed_rows, dims, sums):
    size_x, size_y, size_z = dims
    row_iota = lax.broadcasted_iota(jnp.int32, (size_x * size_z, LANES), 0)
    y_iota = lax.broadcasted_iota(jnp.int32, (size_y, LANES), 0)
    z = cell & (size_z - 1)
    column = cell >> 7
    y = jnp.where(cell >= 0, column & (size_y - 1), size_y)
    line = ((column >> 4) * size_z) | z
    for t in range(GROUP // 2):
        lefts, rights = [], []
        for b in (2 * t, 2 * t + 1):
            mask = y_iota == y[b : b + 1, :]
            lefts.append(
                jnp.concatenate(
                    [
                        jnp.where(mask, fed_rows[c, b : b + 1, :], 0.0).astype(jnp.bfloat16)
                        for c in range(COMPS)
                    ],
                    axis=0,
                )
            )
            rights.append(
                jnp.where(row_iota == line[b : b + 1, :], 1.0, 0.0).astype(jnp.bfloat16)
            )
        unit, stage = t % 2, t // 2
        pltpu.matmul_push_rhs(
            jnp.concatenate(rights, axis=1),
            staging_register=stage,
            mxu_index=unit,
            transpose=True,
        )
        pltpu.matmul_acc_lhs(
            sums[unit], jnp.concatenate(lefts, axis=1), load_staged_rhs=stage
        )


def matrix_probe(cell, lines, dims, sums):
    size_x, size_y, size_z = dims
    row_iota = lax.broadcasted_iota(jnp.int32, (size_x * size_z, LANES), 0)
    y_iota = lax.broadcasted_iota(jnp.int32, (size_y, LANES), 0)
    column = cell >> 7
    y = jnp.where(cell >= 0, column & (size_y - 1), size_y)
    line = ((column >> 4) * size_z) | (cell & (size_z - 1))
    found = [[] for _ in range(COMPS)]
    for t in range(GROUP // 2):
        pair = (2 * t, 2 * t + 1)
        unit, stage = t % 2, t // 2
        pltpu.matmul_push_rhs(
            jnp.concatenate(
                [
                    jnp.where(row_iota == line[b : b + 1, :], 1.0, 0.0).astype(jnp.bfloat16)
                    for b in pair
                ],
                axis=1,
            ),
            staging_register=stage,
            mxu_index=unit,
        )
        pltpu.matmul_acc_lhs(sums[2 * stage + unit], lines[...], load_staged_rhs=stage)
        lifted = pltpu.matmul_pop(sums[2 * stage + unit])
        for i, b in enumerate(pair):
            mask = y_iota == y[b : b + 1, :]
            for c in range(COMPS):
                part = lifted[c * size_y : (c + 1) * size_y, i * LANES : (i + 1) * LANES]
                found[c].append(jnp.sum(jnp.where(mask, part, 0.0), axis=0, keepdims=True))
    return [jnp.concatenate(rows, axis=0) for rows in found]


def coupling_step(slope, partition, dims, refs, load_cell, load, store, span, sums, kept=None):
    size_x, size_y, size_z = dims
    table, plain, lines, fed_rows = refs
    columns = size_x * size_y

    def look(g):
        cell = load_cell(g)
        z = cell & (size_z - 1)
        column = cell >> 7
        words = [jnp.zeros((GROUP, LANES), jnp.int32)] * PAIRS
        single = jnp.zeros((GROUP, LANES), jnp.float32)
        for j in range(columns):
            here = column == j
            for c in range(PAIRS):
                row = jnp.broadcast_to(table[c, j : j + 1, :], (GROUP, LANES))
                words[c] = jnp.where(here, jnp.take_along_axis(row, z, axis=1), words[c])
            row = jnp.broadcast_to(plain[j : j + 1, :], (GROUP, LANES))
            single = jnp.where(here, jnp.take_along_axis(row, z, axis=1), single)
        return (*words, single)

    def work(g, probe, into):
        live = load_cell(g) >= 0
        velo = [load(g, 0), load(g, 1), load(g, 2)]
        radi = load(g, 3)
        under = (
            probe[4] * slope[0] + probe[5] * slope[1] + probe[6] * slope[2]
        ) - probe[3]
        growth = GROW * (jnp.maximum(under, 0.0) + jnp.log1p(jnp.exp(-jnp.abs(under))))
        beta = DRAG / (radi * radi)
        push = -(MOMENT * radi * radi * radi * beta)
        slip = [probe[c] - velo[c] for c in range(3)]
        fed = growth * radi
        sources = [push * slip[c] for c in range(3)] + [LATENT * growth * radi]
        sources += [(1.0 - partition[s]) * probe[4 + s] * fed for s in range(3)]
        new_velo = [velo[c] + beta * slip[c] for c in range(3)]
        new_velo[2] = new_velo[2] - SETTLE * radi
        new_radi = radi + growth / radi
        for c in range(3):
            store(g, c, jnp.where(live, new_velo[c], velo[c]))
        store(g, 3, jnp.where(live, new_radi, radi))
        for c in range(COMPS):
            into[c] = sources[c]
        if kept is not None:
            into[COMPS] = load_cell(g).astype(jnp.float32)

    def spend(g):
        spend_group(load_cell(g), fed_rows, dims, sums)

    first, stop = span
    last = stop - 1

    if kept is None:

        def group(g, found):
            spend(g - 1)
            later = look(jnp.minimum(g + 1, last))
            work(g, unpaired(found), fed_rows)
            return later

        def four(i, found):
            for r in range(4):
                found = group(4 * i + r, found)
            return found

        work(first, unpaired(look(first)), fed_rows)
        found = look(first + 1)
        for r in range(1, 4):
            found = group(first + r, found)
        lax.fori_loop(first // 4 + 1, stop // 4, four, found)
        spend(last)
    else:

        def pair(g):
            return look(g), tuple(matrix_probe(load_cell(g + 1), lines, dims, sums))

        def both(i, found):
            g = 2 * i
            later = pair(jnp.minimum(g + 2, last - 1))
            work(g, unpaired(found[0]), kept.at[g - first])
            work(g + 1, found[1], kept.at[g + 1 - first])
            return later

        def four(i, found):
            return both(2 * i + 1, both(2 * i, found))

        lax.fori_loop(first // 4, stop // 4, four, pair(first))


def deposit_scope(rows, width, body):
    pl.run_scoped(
        lambda *sums: body(sums),
        pltpu.ACC(mxu_id=0)((rows, width), jnp.float32),
        pltpu.ACC(mxu_id=1)((rows, width), jnp.float32),
    )


def fill_lines(lines, value, size_y):
    for c in range(COMPS):
        part = value(c).astype(jnp.bfloat16)
        lines[c * size_y : (c + 1) * size_y, :] = jnp.concatenate(
            [part[x : x + size_y] for x in range(0, part.shape[0], size_y)], axis=1
        )


def fill_table(table, plain, value):
    rounded = [value(c).astype(jnp.bfloat16).astype(jnp.float32) for c in range(COMPS)]
    for c in range(PAIRS):
        table[c] = paired(rounded[c], rounded[PAIRS + 1 + c])
    plain[...] = rounded[PAIRS]


def got_cell(got, g):
    return got[pl.ds(g * (SEND * GROUP) + 4, GROUP, stride=SEND), :].astype(jnp.int32)


def steps_kernel(
    slope, partition, rate, got, melt, low_x, high_x, low_z, high_z,
    back, melt_mid, acc, kept, *refs,
):
    table, plain, lines, _ = refs
    size_y = low_x.shape[1]
    size_x = melt.shape[1] // size_y
    dims = (size_x, size_y, melt.shape[2])
    groups = got.shape[0] // (SEND * GROUP)

    def stay(g, f):
        return pl.ds(g * (BACK * GROUP) + f, GROUP, stride=BACK)

    def store(g, f, value):
        back[stay(g, f), :] = value

    def step(load, share, kept):
        def body(sums):
            coupling_step(
                slope, partition, dims, refs, lambda g: got_cell(got, g), load, store,
                (share, groups), sums,
            )
            acc[...] = pltpu.matmul_pop(sums[0]) + pltpu.matmul_pop(sums[1])

        def keep(*sums):
            coupling_step(
                slope, partition, dims, refs, lambda g: got_cell(got, g), load, store,
                (0, share), sums, kept,
            )

        if share:
            pl.run_scoped(
                keep, *[pltpu.ACC(mxu_id=i % 2)(acc.shape, jnp.float32) for i in range(4)]
            )
        deposit_scope(*acc.shape, body)

    fill_table(table, plain, lambda c: melt[c])
    step(lambda g, f: got[pl.ds(g * (SEND * GROUP) + f, GROUP, stride=SEND), :], 0, None)
    for c in range(COMPS):
        fresh = diffused(melt[c], low_x[c], high_x[c], low_z[c], high_z[c], rate[c])
        melt_mid[c] = fresh + deposit_of(acc, c, size_x, size_y)
    fill_table(table, plain, lambda c: melt_mid[c])
    fill_lines(lines, lambda c: melt_mid[c], size_y)
    step(lambda g, f: back[stay(g, f), :], kept.shape[0], kept)


def kept_kernel(dims, kept, before, acc):

    def body(sums):
        def two(i, _):
            for g in (2 * i, 2 * i + 1):
                spend_group(kept[g, COMPS].astype(jnp.int32), kept.at[g], dims, sums)
            return 0

        lax.fori_loop(0, kept.shape[0] // 2, two, 0)
        acc[...] = before[...] + (pltpu.matmul_pop(sums[0]) + pltpu.matmul_pop(sums[1]))

    deposit_scope(*acc.shape, body)


def finish_kernel(rate, melt, acc, low_x, high_x, low_z, high_z, out):
    size_y = low_x.shape[1]
    size_x = melt.shape[1] // size_y
    for c in range(COMPS):
        fresh = diffused(melt[c], low_x[c], high_x[c], low_z[c], high_z[c], rate[c])
        fresh = fresh + deposit_of(acc, c, size_x, size_y)
        for x in range(size_x):
            out[x, c] = fresh[x * size_y : (x + 1) * size_y]


def kernel_call(kernel, outs, in_specs, out_specs, scratch=(), limit=LIMIT, cost=None):
    return pl.pallas_call(
        kernel,
        out_shape=outs,
        in_specs=in_specs,
        out_specs=out_specs,
        scratch_shapes=list(scratch),
        compiler_params=pltpu.CompilerParams(vmem_limit_bytes=limit),
        cost_estimate=None
        if cost is None
        else pl.CostEstimate(flops=cost, bytes_accessed=2**20, transcendentals=0),
    )


def shape(*dims):
    return jax.ShapeDtypeStruct(dims, jnp.float32)


def neighbours(melt, size_y):
    def swap(low_face, high_face, axis):
        n = lax.axis_size(axis)
        even = lax.axis_index(axis) % 2 == 0

        def meet(face, start):
            pairs = [(i, i + 1) for i in range(start, n - 1, 2)]
            return lax.ppermute(face, axis, pairs + [(j, i) for i, j in pairs])

        first = meet(jnp.where(even, high_face, low_face), 0)
        second = meet(jnp.where(even, low_face, high_face), 1)
        return jnp.where(even, second, first), jnp.where(even, first, second)

    low_x, high_x = swap(melt[:, :size_y, :], melt[:, -size_y:, :], "brick")
    low_z, high_z = swap(melt[:, :, 0], melt[:, :, -1], "sec")
    return low_x, high_x, low_z[:, :, None], high_z[:, :, None]


def run_steps(got, melt, halo, slope, partition, rate, size_y):
    comps, columns, size_z = melt.shape
    size_x = columns // size_y
    slots = got.shape[0] // SEND
    sums = shape(comps * size_y, size_x * size_z)
    return kernel_call(
        steps_kernel,
        (
            shape(slots * BACK, LANES),
            shape(comps, columns, size_z),
            sums,
            shape(slots // GROUP * 3 // 4, comps + 1, GROUP, LANES),
        ),
        [SMEM, SMEM, SMEM] + [VMEM] * 6,
        (VMEM, VMEM, VMEM, VMEM),
        [
            pltpu.VMEM((PAIRS, columns, size_z), jnp.int32),
            pltpu.VMEM((columns, size_z), jnp.float32),
            pltpu.VMEM((comps * size_y, size_x * size_z), jnp.bfloat16),
            pltpu.VMEM((comps, GROUP, LANES), jnp.float32),
        ],
    )(slope, partition, rate, got, melt, *halo)


def run_kept(kept, before, dims):
    return kernel_call(
        functools.partial(kept_kernel, dims),
        shape(*before.shape),
        [VMEM] * 2,
        VMEM,
        cost=8_000_000_000,
    )(kept, before)


def exchange(rows, devices):
    each = rows.shape[0] // CAP
    swapped = lax.all_to_all(
        rows.reshape(each, CAP, LANES), AXES, split_axis=0, concat_axis=0, tiled=True
    )
    return swapped.reshape(rows.shape)


def local(melt, velocity, radius, cell, target, count, slope, partition, rate):
    devices = lax.axis_size(AXES)
    size_x, size_y, comps, size_z = melt.shape
    blocks = target.shape[0]
    slots = devices * CAP
    sent, slot_of = kernel_call(
        pack_kernel,
        (shape(slots * SEND, LANES), jax.ShapeDtypeStruct((blocks,), jnp.int32)),
        [HBM] * 5,
        (VMEM, SMEM),
        [
            pltpu.SMEM((blocks,), jnp.int32),
            pltpu.SMEM((blocks,), jnp.int32),
            pltpu.VMEM((3, blocks, LANES), jnp.float32),
            pltpu.VMEM((blocks, LANES), jnp.float32),
            pltpu.VMEM((blocks, LANES), jnp.int32),
            pltpu.SMEM((devices,), jnp.int32),
            pltpu.SemaphoreType.DMA((5,)),
        ],
        limit=WHOLE,
    )(target, count, jnp.transpose(velocity, (1, 0, 2)), radius, cell)
    got = exchange(sent, devices)
    start = jnp.transpose(melt, (2, 0, 1, 3)).reshape(comps, size_x * size_y, size_z)
    halo = neighbours(start, size_y)
    back, middle, acc, kept = run_steps(got, start, halo, slope, partition, rate, size_y)
    returned = exchange(back, devices)
    halo = neighbours(middle, size_y)
    acc = run_kept(kept, acc, (size_x, size_y, size_z))
    final = kernel_call(
        finish_kernel,
        shape(size_x, comps, size_y, size_z),
        [SMEM] + [VMEM] * 6,
        VMEM,
    )(rate, middle, acc, *halo)
    melt_out = jnp.transpose(final, (0, 2, 1, 3))
    velocity_out, radius_out = kernel_call(
        unpack_kernel,
        (shape(3, blocks, LANES), shape(blocks, LANES)),
        [SMEM, VMEM],
        (HBM, HBM),
        [
            pltpu.VMEM((3, blocks, LANES), jnp.float32),
            pltpu.VMEM((blocks, LANES), jnp.float32),
            pltpu.SemaphoreType.DMA((4,)),
        ],
    )(slot_of, returned)
    return melt_out, jnp.transpose(velocity_out, (1, 0, 2)), radius_out


def solution(mesh):
    return jax.shard_map(
        local,
        mesh=mesh,
        in_specs=(
            P("brick", None, None, "sec"),
            P(AXES, None, None),
            P(AXES, None),
            P(AXES, None),
            P(AXES),
            P(AXES),
            P(),
            P(),
            P(),
        ),
        out_specs=(P("brick", None, None, "sec"), P(AXES, None, None), P(AXES, None)),
        check_vma=False,
    )
```

```python
import functools

import jax
import jax.numpy as jnp
from jax import lax
from jax.experimental import pallas as pl
from jax.experimental.pallas import tpu as pltpu
from jax.sharding import PartitionSpec as P

AXES = ("sec", "brick")
CAP = 4
LANES = 128
COMPS = 7
SEND = 5
BACK = 4
GROUP = 8
PAIRS = 3
TINY = 2.0**-126

GROW = 0.4
DRAG = 0.25
MOMENT = 0.4
LATENT = 0.5
SETTLE = 0.1

VMEM = pl.BlockSpec(memory_space=pltpu.VMEM)
SMEM = pl.BlockSpec(memory_space=pltpu.SMEM)
HBM = pl.BlockSpec(memory_space=pltpu.HBM)
LIMIT = 16 * 2**20
WHOLE = 64 * 2**20


def pack_kernel(
    target_hbm, count_hbm, velo_hbm, radi_hbm, cell_hbm,
    sent, slot_of, target, count, velo, radi, cell, seen, ready,
):
    blocks = radi.shape[0]
    bricks = seen.shape[0]
    pairs = [
        (target_hbm, target),
        (count_hbm, count),
        (velo_hbm, velo),
        (radi_hbm, radi),
        (cell_hbm, cell),
    ]
    copies = [
        pltpu.make_async_copy(source, into, ready.at[i]) for i, (source, into) in enumerate(pairs)
    ]
    for copy in copies:
        copy.start()

    def clear(i, _):
        seen[i] = 0
        return 0

    lax.fori_loop(0, bricks, clear, 0, unroll=16)
    sent[...] = jnp.full(sent.shape, -1.0, jnp.float32)
    lane = lax.broadcasted_iota(jnp.int32, (1, LANES), 1)
    copies[0].wait()

    def rank(k, _):
        brick = target[k]
        earlier = seen[brick]
        seen[brick] = earlier + 1
        slot_of[k] = brick * CAP + earlier
        return 0

    lax.fori_loop(0, blocks, rank, 0, unroll=16)
    for copy in copies[1:]:
        copy.wait()

    def place(k, _):
        row = slot_of[k] * SEND
        for c in range(3):
            sent[pl.ds(row + c, 1), :] = velo[c, pl.ds(k, 1), :]
        sent[pl.ds(row + 3, 1), :] = radi[pl.ds(k, 1), :]
        where = cell[pl.ds(k, 1), :].astype(jnp.float32)
        sent[pl.ds(row + 4, 1), :] = jnp.where(lane < count[k], where, -1.0)
        return 0

    lax.fori_loop(0, blocks, place, 0, unroll=8)


def unpack_kernel(slot_of, back, velo_hbm, radi_hbm, velo, radi, done):
    blocks = radi.shape[0]
    half = blocks // 2

    def place(k, _):
        row = slot_of[k] * BACK
        for c in range(3):
            velo[c, pl.ds(k, 1), :] = back[pl.ds(row + c, 1), :]
        radi[pl.ds(k, 1), :] = back[pl.ds(row + 3, 1), :]
        return 0

    copies = []
    for part in range(2):
        lax.fori_loop(part * half, (part + 1) * half, place, 0, unroll=8)
        own = pl.ds(part * half, half)
        copies += [
            pltpu.make_async_copy(velo.at[:, own], velo_hbm.at[:, own], done.at[2 * part]),
            pltpu.make_async_copy(radi.at[own], radi_hbm.at[own], done.at[2 * part + 1]),
        ]
        copies[-2].start()
        copies[-1].start()
    for copy in copies:
        copy.wait()


def diffused(melt, low_x, high_x, low_z, high_z, rate):
    rows, size_z = melt.shape
    size_y = low_x.shape[0]
    lane = lax.broadcasted_iota(jnp.int32, (rows, size_z), 1)
    level = lax.broadcasted_iota(jnp.int32, (rows, size_z), 0) % size_y
    below_x = jnp.concatenate([low_x, melt[:-size_y]], axis=0)
    above_x = jnp.concatenate([melt[size_y:], high_x], axis=0)
    below_y = jnp.where(level == 0, 0.0, pltpu.roll(melt, 1, 0))
    above_y = jnp.where(level == size_y - 1, 0.0, pltpu.roll(melt, rows - 1, 0))
    below_z = jnp.where(lane == 0, low_z, pltpu.roll(melt, 1, 1))
    above_z = jnp.where(lane == size_z - 1, high_z, pltpu.roll(melt, size_z - 1, 1))
    beside = above_x + below_x + above_y + below_y + above_z + below_z
    return melt + rate * (beside - 6.0 * melt)


def deposit_of(acc, comp, size_x, size_y):
    part = acc[comp * size_y : (comp + 1) * size_y, :]
    size_z = part.shape[1] // size_x
    return jnp.concatenate(
        [part[:, x * size_z : (x + 1) * size_z] for x in range(size_x)], axis=0
    )


def code_of(value):
    size = jnp.abs(value)
    exponent = jnp.floor(jnp.log2(jnp.maximum(size, TINY)))
    mantissa = size * power(-exponent)
    high = mantissa >= 2.0
    low = mantissa < 1.0
    exponent = jnp.where(high, exponent + 1.0, jnp.where(low, exponent - 1.0, exponent))
    mantissa = jnp.where(high, mantissa * 0.5, jnp.where(low, mantissa * 2.0, mantissa))
    code = (exponent + 126.0) * 128.0 + mantissa * 128.0
    code = jnp.where(size < TINY, 0.0, code)
    return jnp.where(value < 0.0, -code, code).astype(jnp.int32)


def value_of(code):
    size = jnp.abs(code)
    scale = power((size >> 7).astype(jnp.float32) - 127.0)
    value = ((size & 127) + 128).astype(jnp.float32) * (1.0 / 128.0) * scale
    value = jnp.where(size == 0, 0.0, value)
    return jnp.where(code < 0, -value, value)


def power(exponent):
    return jnp.exp2(exponent).astype(jnp.bfloat16).astype(jnp.float32)


def paired(high, low):
    return code_of(high) * 65536 + (code_of(low) & 65535)


def unpaired(found):
    first = [value_of(word >> 16) for word in found[:PAIRS]]
    second = [value_of((word << 16) >> 16) for word in found[:PAIRS]]
    return [*first, found[PAIRS], *second]


def spend_group(cell, fed_rows, dims, sums):
    size_x, size_y, size_z = dims
    row_iota = lax.broadcasted_iota(jnp.int32, (size_x * size_z, LANES), 0)
    y_iota = lax.broadcasted_iota(jnp.int32, (size_y, LANES), 0)
    z = cell & (size_z - 1)
    column = cell >> 7
    y = jnp.where(cell >= 0, column & (size_y - 1), size_y)
    line = ((column >> 4) * size_z) | z
    for t in range(GROUP // 2):
        lefts, rights = [], []
        for b in (2 * t, 2 * t + 1):
            mask = y_iota == y[b : b + 1, :]
            lefts.append(
                jnp.concatenate(
                    [
                        jnp.where(mask, fed_rows[c, b : b + 1, :], 0.0).astype(jnp.bfloat16)
                        for c in range(COMPS)
                    ],
                    axis=0,
                )
            )
            rights.append(
                jnp.where(row_iota == line[b : b + 1, :], 1.0, 0.0).astype(jnp.bfloat16)
            )
        unit, stage = t % 2, t // 2
        pltpu.matmul_push_rhs(
            jnp.concatenate(rights, axis=1),
            staging_register=stage,
            mxu_index=unit,
            transpose=True,
        )
        pltpu.matmul_acc_lhs(
            sums[unit], jnp.concatenate(lefts, axis=1), load_staged_rhs=stage
        )


def matrix_probe(cell, lines, dims, sums):
    size_x, size_y, size_z = dims
    row_iota = lax.broadcasted_iota(jnp.int32, (size_x * size_z, LANES), 0)
    y_iota = lax.broadcasted_iota(jnp.int32, (size_y, LANES), 0)
    column = cell >> 7
    y = jnp.where(cell >= 0, column & (size_y - 1), size_y)
    line = ((column >> 4) * size_z) | (cell & (size_z - 1))
    found = [[] for _ in range(COMPS)]
    for t in range(GROUP // 2):
        pair = (2 * t, 2 * t + 1)
        unit, stage = t % 2, t // 2
        pltpu.matmul_push_rhs(
            jnp.concatenate(
                [
                    jnp.where(row_iota == line[b : b + 1, :], 1.0, 0.0).astype(jnp.bfloat16)
                    for b in pair
                ],
                axis=1,
            ),
            staging_register=stage,
            mxu_index=unit,
        )
        pltpu.matmul_acc_lhs(sums[2 * stage + unit], lines[...], load_staged_rhs=stage)
        lifted = pltpu.matmul_pop(sums[2 * stage + unit])
        for i, b in enumerate(pair):
            mask = y_iota == y[b : b + 1, :]
            for c in range(COMPS):
                part = lifted[c * size_y : (c + 1) * size_y, i * LANES : (i + 1) * LANES]
                found[c].append(jnp.sum(jnp.where(mask, part, 0.0), axis=0, keepdims=True))
    return [jnp.concatenate(rows, axis=0) for rows in found]


def coupling_step(slope, partition, dims, refs, load_cell, load, store, span, sums, kept=None):
    size_x, size_y, size_z = dims
    table, plain, lines, fed_rows = refs
    columns = size_x * size_y

    def look(g):
        cell = load_cell(g)
        z = cell & (size_z - 1)
        column = cell >> 7
        words = [jnp.zeros((GROUP, LANES), jnp.int32)] * PAIRS
        single = jnp.zeros((GROUP, LANES), jnp.float32)
        for j in range(columns):
            here = column == j
            for c in range(PAIRS):
                row = jnp.broadcast_to(table[c, j : j + 1, :], (GROUP, LANES))
                words[c] = jnp.where(here, jnp.take_along_axis(row, z, axis=1), words[c])
            row = jnp.broadcast_to(plain[j : j + 1, :], (GROUP, LANES))
            single = jnp.where(here, jnp.take_along_axis(row, z, axis=1), single)
        return (*words, single)

    def work(g, probe, into):
        live = load_cell(g) >= 0
        velo = [load(g, 0), load(g, 1), load(g, 2)]
        radi = load(g, 3)
        under = (
            probe[4] * slope[0] + probe[5] * slope[1] + probe[6] * slope[2]
        ) - probe[3]
        growth = GROW * (jnp.maximum(under, 0.0) + jnp.log1p(jnp.exp(-jnp.abs(under))))
        beta = DRAG / (radi * radi)
        push = -(MOMENT * radi * radi * radi * beta)
        slip = [probe[c] - velo[c] for c in range(3)]
        fed = growth * radi
        sources = [push * slip[c] for c in range(3)] + [LATENT * growth * radi]
        sources += [(1.0 - partition[s]) * probe[4 + s] * fed for s in range(3)]
        new_velo = [velo[c] + beta * slip[c] for c in range(3)]
        new_velo[2] = new_velo[2] - SETTLE * radi
        new_radi = radi + growth / radi
        for c in range(3):
            store(g, c, jnp.where(live, new_velo[c], velo[c]))
        store(g, 3, jnp.where(live, new_radi, radi))
        for c in range(COMPS):
            into[c] = sources[c]
        if kept is not None:
            into[COMPS] = load_cell(g).astype(jnp.float32)

    def spend(g):
        spend_group(load_cell(g), fed_rows, dims, sums)

    first, stop = span
    last = stop - 1

    if kept is None:

        def group(g, found):
            spend(g - 1)
            later = look(jnp.minimum(g + 1, last))
            work(g, unpaired(found), fed_rows)
            return later

        def four(i, found):
            for r in range(4):
                found = group(4 * i + r, found)
            return found

        work(first, unpaired(look(first)), fed_rows)
        found = look(first + 1)
        for r in range(1, 4):
            found = group(first + r, found)
        lax.fori_loop(first // 4 + 1, stop // 4, four, found)
        spend(last)
    else:

        def pair(g):
            return look(g), tuple(matrix_probe(load_cell(g + 1), lines, dims, sums))

        def both(i, found):
            g = 2 * i
            later = pair(jnp.minimum(g + 2, last - 1))
            work(g, unpaired(found[0]), kept.at[g - first])
            work(g + 1, found[1], kept.at[g + 1 - first])
            return later

        def four(i, found):
            return both(2 * i + 1, both(2 * i, found))

        lax.fori_loop(first // 4, stop // 4, four, pair(first))


def deposit_scope(rows, width, body):
    pl.run_scoped(
        lambda *sums: body(sums),
        pltpu.ACC(mxu_id=0)((rows, width), jnp.float32),
        pltpu.ACC(mxu_id=1)((rows, width), jnp.float32),
    )


def fill_lines(lines, value, size_y):
    for c in range(COMPS):
        part = value(c).astype(jnp.bfloat16)
        lines[c * size_y : (c + 1) * size_y, :] = jnp.concatenate(
            [part[x : x + size_y] for x in range(0, part.shape[0], size_y)], axis=1
        )


def fill_table(table, plain, value):
    rounded = [value(c).astype(jnp.bfloat16).astype(jnp.float32) for c in range(COMPS)]
    for c in range(PAIRS):
        table[c] = paired(rounded[c], rounded[PAIRS + 1 + c])
    plain[...] = rounded[PAIRS]


def got_cell(got, g):
    return got[pl.ds(g * (SEND * GROUP) + 4, GROUP, stride=SEND), :].astype(jnp.int32)


def steps_kernel(
    slope, partition, rate, got, melt, low_x, high_x, low_z, high_z,
    back, melt_mid, acc, kept, *refs,
):
    table, plain, lines, _ = refs
    size_y = low_x.shape[1]
    size_x = melt.shape[1] // size_y
    dims = (size_x, size_y, melt.shape[2])
    groups = got.shape[0] // (SEND * GROUP)

    def stay(g, f):
        return pl.ds(g * (BACK * GROUP) + f, GROUP, stride=BACK)

    def store(g, f, value):
        back[stay(g, f), :] = value

    def step(load, share, kept):
        def body(sums):
            coupling_step(
                slope, partition, dims, refs, lambda g: got_cell(got, g), load, store,
                (share, groups), sums,
            )
            acc[...] = pltpu.matmul_pop(sums[0]) + pltpu.matmul_pop(sums[1])

        def keep(*sums):
            coupling_step(
                slope, partition, dims, refs, lambda g: got_cell(got, g), load, store,
                (0, share), sums, kept,
            )

        if share:
            pl.run_scoped(
                keep, *[pltpu.ACC(mxu_id=i % 2)(acc.shape, jnp.float32) for i in range(4)]
            )
        deposit_scope(*acc.shape, body)

    fill_table(table, plain, lambda c: melt[c])
    step(lambda g, f: got[pl.ds(g * (SEND * GROUP) + f, GROUP, stride=SEND), :], 0, None)
    for c in range(COMPS):
        fresh = diffused(melt[c], low_x[c], high_x[c], low_z[c], high_z[c], rate[c])
        melt_mid[c] = fresh + deposit_of(acc, c, size_x, size_y)
    fill_table(table, plain, lambda c: melt_mid[c])
    fill_lines(lines, lambda c: melt_mid[c], size_y)
    step(lambda g, f: back[stay(g, f), :], kept.shape[0], kept)


def kept_kernel(dims, kept, before, acc):

    def body(sums):
        def two(i, _):
            for g in (2 * i, 2 * i + 1):
                spend_group(kept[g, COMPS].astype(jnp.int32), kept.at[g], dims, sums)
            return 0

        lax.fori_loop(0, kept.shape[0] // 2, two, 0)
        acc[...] = before[...] + (pltpu.matmul_pop(sums[0]) + pltpu.matmul_pop(sums[1]))

    deposit_scope(*acc.shape, body)


def finish_kernel(rate, melt, acc, low_x, high_x, low_z, high_z, out):
    size_y = low_x.shape[1]
    size_x = melt.shape[1] // size_y
    for c in range(COMPS):
        fresh = diffused(melt[c], low_x[c], high_x[c], low_z[c], high_z[c], rate[c])
        fresh = fresh + deposit_of(acc, c, size_x, size_y)
        for x in range(size_x):
            out[x, c] = fresh[x * size_y : (x + 1) * size_y]


def kernel_call(kernel, outs, in_specs, out_specs, scratch=(), limit=LIMIT, cost=None):
    return pl.pallas_call(
        kernel,
        out_shape=outs,
        in_specs=in_specs,
        out_specs=out_specs,
        scratch_shapes=list(scratch),
        compiler_params=pltpu.CompilerParams(vmem_limit_bytes=limit),
        cost_estimate=None
        if cost is None
        else pl.CostEstimate(flops=cost, bytes_accessed=2**20, transcendentals=0),
    )


def shape(*dims):
    return jax.ShapeDtypeStruct(dims, jnp.float32)


def neighbours(melt, size_y):
    def swap(low_face, high_face, axis):
        n = lax.axis_size(axis)
        even = lax.axis_index(axis) % 2 == 0

        def meet(face, start):
            pairs = [(i, i + 1) for i in range(start, n - 1, 2)]
            return lax.ppermute(face, axis, pairs + [(j, i) for i, j in pairs])

        first = meet(jnp.where(even, high_face, low_face), 0)
        second = meet(jnp.where(even, low_face, high_face), 1)
        return jnp.where(even, second, first), jnp.where(even, first, second)

    low_x, high_x = swap(melt[:, :size_y, :], melt[:, -size_y:, :], "brick")
    low_z, high_z = swap(melt[:, :, 0], melt[:, :, -1], "sec")
    return low_x, high_x, low_z[:, :, None], high_z[:, :, None]


def run_steps(got, melt, halo, slope, partition, rate, size_y):
    comps, columns, size_z = melt.shape
    size_x = columns // size_y
    slots = got.shape[0] // SEND
    sums = shape(comps * size_y, size_x * size_z)
    return kernel_call(
        steps_kernel,
        (
            shape(slots * BACK, LANES),
            shape(comps, columns, size_z),
            sums,
            shape(slots // GROUP * 5 // 8, comps + 1, GROUP, LANES),
        ),
        [SMEM, SMEM, SMEM] + [VMEM] * 6,
        (VMEM, VMEM, VMEM, VMEM),
        [
            pltpu.VMEM((PAIRS, columns, size_z), jnp.int32),
            pltpu.VMEM((columns, size_z), jnp.float32),
            pltpu.VMEM((comps * size_y, size_x * size_z), jnp.bfloat16),
            pltpu.VMEM((comps, GROUP, LANES), jnp.float32),
        ],
    )(slope, partition, rate, got, melt, *halo)


def run_kept(kept, before, dims):
    return kernel_call(
        functools.partial(kept_kernel, dims),
        shape(*before.shape),
        [VMEM] * 2,
        VMEM,
        cost=8_000_000_000,
    )(kept, before)


def exchange(rows, devices):
    each = rows.shape[0] // CAP
    swapped = lax.all_to_all(
        rows.reshape(each, CAP, LANES), AXES, split_axis=0, concat_axis=0, tiled=True
    )
    return swapped.reshape(rows.shape)


def local(melt, velocity, radius, cell, target, count, slope, partition, rate):
    devices = lax.axis_size(AXES)
    size_x, size_y, comps, size_z = melt.shape
    blocks = target.shape[0]
    slots = devices * CAP
    sent, slot_of = kernel_call(
        pack_kernel,
        (shape(slots * SEND, LANES), jax.ShapeDtypeStruct((blocks,), jnp.int32)),
        [HBM] * 5,
        (VMEM, SMEM),
        [
            pltpu.SMEM((blocks,), jnp.int32),
            pltpu.SMEM((blocks,), jnp.int32),
            pltpu.VMEM((3, blocks, LANES), jnp.float32),
            pltpu.VMEM((blocks, LANES), jnp.float32),
            pltpu.VMEM((blocks, LANES), jnp.int32),
            pltpu.SMEM((devices,), jnp.int32),
            pltpu.SemaphoreType.DMA((5,)),
        ],
        limit=WHOLE,
    )(target, count, jnp.transpose(velocity, (1, 0, 2)), radius, cell)
    got = exchange(sent, devices)
    start = jnp.transpose(melt, (2, 0, 1, 3)).reshape(comps, size_x * size_y, size_z)
    halo = neighbours(start, size_y)
    back, middle, acc, kept = run_steps(got, start, halo, slope, partition, rate, size_y)
    returned = exchange(back, devices)
    halo = neighbours(middle, size_y)
    acc = run_kept(kept, acc, (size_x, size_y, size_z))
    final = kernel_call(
        finish_kernel,
        shape(size_x, comps, size_y, size_z),
        [SMEM] + [VMEM] * 6,
        VMEM,
    )(rate, middle, acc, *halo)
    melt_out = jnp.transpose(final, (0, 2, 1, 3))
    velocity_out, radius_out = kernel_call(
        unpack_kernel,
        (shape(3, blocks, LANES), shape(blocks, LANES)),
        [SMEM, VMEM],
        (HBM, HBM),
        [
            pltpu.VMEM((3, blocks, LANES), jnp.float32),
            pltpu.VMEM((blocks, LANES), jnp.float32),
            pltpu.SemaphoreType.DMA((4,)),
        ],
    )(slot_of, returned)
    return melt_out, jnp.transpose(velocity_out, (1, 0, 2)), radius_out


def solution(mesh):
    return jax.shard_map(
        local,
        mesh=mesh,
        in_specs=(
            P("brick", None, None, "sec"),
            P(AXES, None, None),
            P(AXES, None),
            P(AXES, None),
            P(AXES),
            P(AXES),
            P(),
            P(),
            P(),
        ),
        out_specs=(P("brick", None, None, "sec"), P(AXES, None, None), P(AXES, None)),
        check_vma=False,
    )
```

```python
import functools

import jax
import jax.numpy as jnp
from jax import lax
from jax.experimental import pallas as pl
from jax.experimental.pallas import tpu as pltpu
from jax.sharding import PartitionSpec as P

AXES = ("sec", "brick")
CAP = 4
LANES = 128
COMPS = 7
SEND = 5
BACK = 4
GROUP = 8
PAIRS = 3
TINY = 2.0**-126

GROW = 0.4
DRAG = 0.25
MOMENT = 0.4
LATENT = 0.5
SETTLE = 0.1

VMEM = pl.BlockSpec(memory_space=pltpu.VMEM)
SMEM = pl.BlockSpec(memory_space=pltpu.SMEM)
HBM = pl.BlockSpec(memory_space=pltpu.HBM)
LIMIT = 16 * 2**20
WHOLE = 64 * 2**20


def pack_kernel(
    target_hbm, count_hbm, velo_hbm, radi_hbm, cell_hbm,
    sent, slot_of, target, count, velo, radi, cell, seen, ready,
):
    blocks = radi.shape[0]
    bricks = seen.shape[0]
    pairs = [
        (target_hbm, target),
        (count_hbm, count),
        (velo_hbm, velo),
        (radi_hbm, radi),
        (cell_hbm, cell),
    ]
    copies = [
        pltpu.make_async_copy(source, into, ready.at[i]) for i, (source, into) in enumerate(pairs)
    ]
    for copy in copies:
        copy.start()

    def clear(i, _):
        seen[i] = 0
        return 0

    lax.fori_loop(0, bricks, clear, 0, unroll=16)
    sent[...] = jnp.full(sent.shape, -1.0, jnp.float32)
    lane = lax.broadcasted_iota(jnp.int32, (1, LANES), 1)
    copies[0].wait()

    def rank(k, _):
        brick = target[k]
        earlier = seen[brick]
        seen[brick] = earlier + 1
        slot_of[k] = brick * CAP + earlier
        return 0

    lax.fori_loop(0, blocks, rank, 0, unroll=16)
    for copy in copies[1:]:
        copy.wait()

    def place(k, _):
        row = slot_of[k] * SEND
        for c in range(3):
            sent[pl.ds(row + c, 1), :] = velo[c, pl.ds(k, 1), :]
        sent[pl.ds(row + 3, 1), :] = radi[pl.ds(k, 1), :]
        where = cell[pl.ds(k, 1), :].astype(jnp.float32)
        sent[pl.ds(row + 4, 1), :] = jnp.where(lane < count[k], where, -1.0)
        return 0

    lax.fori_loop(0, blocks, place, 0, unroll=8)


def unpack_kernel(slot_of, back, velo_hbm, radi_hbm, velo, radi, done):
    blocks = radi.shape[0]
    share = blocks // 4

    def place(k, _):
        row = slot_of[k] * BACK
        for c in range(3):
            velo[c, pl.ds(k, 1), :] = back[pl.ds(row + c, 1), :]
        radi[pl.ds(k, 1), :] = back[pl.ds(row + 3, 1), :]
        return 0

    copies = []
    for part in range(4):
        lax.fori_loop(part * share, (part + 1) * share, place, 0, unroll=8)
        own = pl.ds(part * share, share)
        copies += [
            pltpu.make_async_copy(velo.at[:, own], velo_hbm.at[:, own], done.at[2 * part]),
            pltpu.make_async_copy(radi.at[own], radi_hbm.at[own], done.at[2 * part + 1]),
        ]
        copies[-2].start()
        copies[-1].start()
    for copy in copies:
        copy.wait()


def diffused(melt, low_x, high_x, low_z, high_z, rate):
    rows, size_z = melt.shape
    size_y = low_x.shape[0]
    lane = lax.broadcasted_iota(jnp.int32, (rows, size_z), 1)
    level = lax.broadcasted_iota(jnp.int32, (rows, size_z), 0) % size_y
    below_x = jnp.concatenate([low_x, melt[:-size_y]], axis=0)
    above_x = jnp.concatenate([melt[size_y:], high_x], axis=0)
    below_y = jnp.where(level == 0, 0.0, pltpu.roll(melt, 1, 0))
    above_y = jnp.where(level == size_y - 1, 0.0, pltpu.roll(melt, rows - 1, 0))
    below_z = jnp.where(lane == 0, low_z, pltpu.roll(melt, 1, 1))
    above_z = jnp.where(lane == size_z - 1, high_z, pltpu.roll(melt, size_z - 1, 1))
    beside = above_x + below_x + above_y + below_y + above_z + below_z
    return melt + rate * (beside - 6.0 * melt)


def deposit_of(acc, comp, size_x, size_y):
    part = acc[comp * size_y : (comp + 1) * size_y, :]
    size_z = part.shape[1] // size_x
    return jnp.concatenate(
        [part[:, x * size_z : (x + 1) * size_z] for x in range(size_x)], axis=0
    )


def code_of(value):
    size = jnp.abs(value)
    exponent = jnp.floor(jnp.log2(jnp.maximum(size, TINY)))
    mantissa = size * power(-exponent)
    high = mantissa >= 2.0
    low = mantissa < 1.0
    exponent = jnp.where(high, exponent + 1.0, jnp.where(low, exponent - 1.0, exponent))
    mantissa = jnp.where(high, mantissa * 0.5, jnp.where(low, mantissa * 2.0, mantissa))
    code = (exponent + 126.0) * 128.0 + mantissa * 128.0
    code = jnp.where(size < TINY, 0.0, code)
    return jnp.where(value < 0.0, -code, code).astype(jnp.int32)


def value_of(code):
    size = jnp.abs(code)
    scale = power((size >> 7).astype(jnp.float32) - 127.0)
    value = ((size & 127) + 128).astype(jnp.float32) * (1.0 / 128.0) * scale
    value = jnp.where(size == 0, 0.0, value)
    return jnp.where(code < 0, -value, value)


def power(exponent):
    return jnp.exp2(exponent).astype(jnp.bfloat16).astype(jnp.float32)


def paired(high, low):
    return code_of(high) * 65536 + (code_of(low) & 65535)


def unpaired(found):
    first = [value_of(word >> 16) for word in found[:PAIRS]]
    second = [value_of((word << 16) >> 16) for word in found[:PAIRS]]
    return [*first, found[PAIRS], *second]


def spend_group(cell, fed_rows, dims, sums):
    size_x, size_y, size_z = dims
    row_iota = lax.broadcasted_iota(jnp.int32, (size_x * size_z, LANES), 0)
    y_iota = lax.broadcasted_iota(jnp.int32, (size_y, LANES), 0)
    z = cell & (size_z - 1)
    column = cell >> 7
    y = jnp.where(cell >= 0, column & (size_y - 1), size_y)
    line = ((column >> 4) * size_z) | z
    for t in range(GROUP // 2):
        lefts, rights = [], []
        for b in (2 * t, 2 * t + 1):
            mask = y_iota == y[b : b + 1, :]
            lefts.append(
                jnp.concatenate(
                    [
                        jnp.where(mask, fed_rows[c, b : b + 1, :], 0.0).astype(jnp.bfloat16)
                        for c in range(COMPS)
                    ],
                    axis=0,
                )
            )
            rights.append(
                jnp.where(row_iota == line[b : b + 1, :], 1.0, 0.0).astype(jnp.bfloat16)
            )
        unit, stage = t % 2, t // 2
        pltpu.matmul_push_rhs(
            jnp.concatenate(rights, axis=1),
            staging_register=stage,
            mxu_index=unit,
            transpose=True,
        )
        pltpu.matmul_acc_lhs(
            sums[unit], jnp.concatenate(lefts, axis=1), load_staged_rhs=stage
        )


def row_sums(parts):
    row = lax.broadcasted_iota(jnp.int32, parts[0].shape, 0)
    width = len(parts) // 2
    while width:
        lower = row % (2 * width) < width
        parts = [
            jnp.where(lower, first, second)
            + jnp.where(
                lower,
                pltpu.roll(first, GROUP - width, 0),
                pltpu.roll(second, width, 0),
            )
            for first, second in zip(parts[:width], parts[width:])
        ]
        width //= 2
    return parts[0]


def matrix_probe(cell, lines, dims, sums):
    size_x, size_y, size_z = dims
    row_iota = lax.broadcasted_iota(jnp.int32, (size_x * size_z, LANES), 0)
    y_iota = lax.broadcasted_iota(jnp.int32, (size_y, LANES), 0)
    column = cell >> 7
    y = jnp.where(cell >= 0, column & (size_y - 1), size_y)
    line = ((column >> 4) * size_z) | (cell & (size_z - 1))
    found = [[] for _ in range(COMPS)]
    for t in range(GROUP // 2):
        pair = (2 * t, 2 * t + 1)
        unit, stage = t % 2, t // 2
        pltpu.matmul_push_rhs(
            jnp.concatenate(
                [
                    jnp.where(row_iota == line[b : b + 1, :], 1.0, 0.0).astype(jnp.bfloat16)
                    for b in pair
                ],
                axis=1,
            ),
            staging_register=stage,
            mxu_index=unit,
        )
        pltpu.matmul_acc_lhs(sums[2 * stage + unit], lines[...], load_staged_rhs=stage)
        lifted = pltpu.matmul_pop(sums[2 * stage + unit])
        for i, b in enumerate(pair):
            mask = y_iota == y[b : b + 1, :]
            for c in range(COMPS):
                part = lifted[c * size_y : (c + 1) * size_y, i * LANES : (i + 1) * LANES]
                part = jnp.where(mask, part, 0.0)
                found[c].append(sum(part[r : r + GROUP] for r in range(0, size_y, GROUP)))
    return [row_sums(parts) for parts in found]


def coupling_step(slope, partition, dims, refs, load_cell, load, store, span, sums, kept=None):
    size_x, size_y, size_z = dims
    table, plain, lines, fed_rows = refs
    columns = size_x * size_y

    def look(g):
        cell = load_cell(g)
        z = cell & (size_z - 1)
        column = cell >> 7
        words = [jnp.zeros((GROUP, LANES), jnp.int32)] * PAIRS
        single = jnp.zeros((GROUP, LANES), jnp.float32)
        for j in range(columns):
            here = column == j
            for c in range(PAIRS):
                row = jnp.broadcast_to(table[c, j : j + 1, :], (GROUP, LANES))
                words[c] = jnp.where(here, jnp.take_along_axis(row, z, axis=1), words[c])
            row = jnp.broadcast_to(plain[j : j + 1, :], (GROUP, LANES))
            single = jnp.where(here, jnp.take_along_axis(row, z, axis=1), single)
        return (*words, single)

    def work(g, probe, into):
        live = load_cell(g) >= 0
        velo = [load(g, 0), load(g, 1), load(g, 2)]
        radi = load(g, 3)
        under = (
            probe[4] * slope[0] + probe[5] * slope[1] + probe[6] * slope[2]
        ) - probe[3]
        growth = GROW * (jnp.maximum(under, 0.0) + jnp.log1p(jnp.exp(-jnp.abs(under))))
        beta = DRAG / (radi * radi)
        push = -(MOMENT * radi * radi * radi * beta)
        slip = [probe[c] - velo[c] for c in range(3)]
        fed = growth * radi
        sources = [push * slip[c] for c in range(3)] + [LATENT * growth * radi]
        sources += [(1.0 - partition[s]) * probe[4 + s] * fed for s in range(3)]
        new_velo = [velo[c] + beta * slip[c] for c in range(3)]
        new_velo[2] = new_velo[2] - SETTLE * radi
        new_radi = radi + growth / radi
        for c in range(3):
            store(g, c, jnp.where(live, new_velo[c], velo[c]))
        store(g, 3, jnp.where(live, new_radi, radi))
        for c in range(COMPS):
            into[c] = sources[c]
        if kept is not None:
            into[COMPS] = load_cell(g).astype(jnp.float32)

    def spend(g):
        spend_group(load_cell(g), fed_rows, dims, sums)

    first, stop = span
    last = stop - 1

    if kept is None:

        def group(g, found):
            spend(g - 1)
            later = look(jnp.minimum(g + 1, last))
            work(g, unpaired(found), fed_rows)
            return later

        def four(i, found):
            for r in range(4):
                found = group(4 * i + r, found)
            return found

        work(first, unpaired(look(first)), fed_rows)
        found = look(first + 1)
        for r in range(1, 4):
            found = group(first + r, found)
        lax.fori_loop(first // 4 + 1, stop // 4, four, found)
        spend(last)
    else:

        def pair(g):
            return look(g), tuple(matrix_probe(load_cell(g + 1), lines, dims, sums))

        def both(i, found):
            g = 2 * i
            later = pair(jnp.minimum(g + 2, last - 1))
            work(g, unpaired(found[0]), kept.at[g - first])
            work(g + 1, found[1], kept.at[g + 1 - first])
            return later

        def four(i, found):
            return both(2 * i + 1, both(2 * i, found))

        lax.fori_loop(first // 4, stop // 4, four, pair(first))


def deposit_scope(rows, width, body):
    pl.run_scoped(
        lambda *sums: body(sums),
        pltpu.ACC(mxu_id=0)((rows, width), jnp.float32),
        pltpu.ACC(mxu_id=1)((rows, width), jnp.float32),
    )


def fill_lines(lines, value, size_y):
    for c in range(COMPS):
        part = value(c).astype(jnp.bfloat16)
        lines[c * size_y : (c + 1) * size_y, :] = jnp.concatenate(
            [part[x : x + size_y] for x in range(0, part.shape[0], size_y)], axis=1
        )


def fill_table(table, plain, value):
    rounded = [value(c).astype(jnp.bfloat16).astype(jnp.float32) for c in range(COMPS)]
    for c in range(PAIRS):
        table[c] = paired(rounded[c], rounded[PAIRS + 1 + c])
    plain[...] = rounded[PAIRS]


def got_cell(got, g):
    return got[pl.ds(g * (SEND * GROUP) + 4, GROUP, stride=SEND), :].astype(jnp.int32)


def steps_kernel(
    slope, partition, rate, got, melt, low_x, high_x, low_z, high_z,
    back, melt_mid, acc, kept, *refs,
):
    table, plain, lines, _ = refs
    size_y = low_x.shape[1]
    size_x = melt.shape[1] // size_y
    dims = (size_x, size_y, melt.shape[2])
    groups = got.shape[0] // (SEND * GROUP)

    def stay(g, f):
        return pl.ds(g * (BACK * GROUP) + f, GROUP, stride=BACK)

    def store(g, f, value):
        back[stay(g, f), :] = value

    def step(load, share, kept):
        def body(sums):
            coupling_step(
                slope, partition, dims, refs, lambda g: got_cell(got, g), load, store,
                (share, groups), sums,
            )
            acc[...] = pltpu.matmul_pop(sums[0]) + pltpu.matmul_pop(sums[1])

        def keep(*sums):
            coupling_step(
                slope, partition, dims, refs, lambda g: got_cell(got, g), load, store,
                (0, share), sums, kept,
            )

        if share:
            pl.run_scoped(
                keep, *[pltpu.ACC(mxu_id=i % 2)(acc.shape, jnp.float32) for i in range(4)]
            )
        deposit_scope(*acc.shape, body)

    fill_table(table, plain, lambda c: melt[c])
    step(lambda g, f: got[pl.ds(g * (SEND * GROUP) + f, GROUP, stride=SEND), :], 0, None)
    for c in range(COMPS):
        fresh = diffused(melt[c], low_x[c], high_x[c], low_z[c], high_z[c], rate[c])
        melt_mid[c] = fresh + deposit_of(acc, c, size_x, size_y)
    fill_table(table, plain, lambda c: melt_mid[c])
    fill_lines(lines, lambda c: melt_mid[c], size_y)
    step(lambda g, f: back[stay(g, f), :], kept.shape[0], kept)


def kept_kernel(dims, kept, before, acc):

    def body(sums):
        def two(i, _):
            for g in (2 * i, 2 * i + 1):
                spend_group(kept[g, COMPS].astype(jnp.int32), kept.at[g], dims, sums)
            return 0

        lax.fori_loop(0, kept.shape[0] // 2, two, 0)
        acc[...] = before[...] + (pltpu.matmul_pop(sums[0]) + pltpu.matmul_pop(sums[1]))

    deposit_scope(*acc.shape, body)


def finish_kernel(rate, melt, acc, low_x, high_x, low_z, high_z, out):
    size_y = low_x.shape[1]
    size_x = melt.shape[1] // size_y
    for c in range(COMPS):
        fresh = diffused(melt[c], low_x[c], high_x[c], low_z[c], high_z[c], rate[c])
        fresh = fresh + deposit_of(acc, c, size_x, size_y)
        for x in range(size_x):
            out[x, c] = fresh[x * size_y : (x + 1) * size_y]


def kernel_call(kernel, outs, in_specs, out_specs, scratch=(), limit=LIMIT, cost=None):
    return pl.pallas_call(
        kernel,
        out_shape=outs,
        in_specs=in_specs,
        out_specs=out_specs,
        scratch_shapes=list(scratch),
        compiler_params=pltpu.CompilerParams(vmem_limit_bytes=limit),
        cost_estimate=None
        if cost is None
        else pl.CostEstimate(flops=cost, bytes_accessed=2**20, transcendentals=0),
    )


def shape(*dims):
    return jax.ShapeDtypeStruct(dims, jnp.float32)


def neighbours(melt, size_y):
    def swap(low_face, high_face, axis):
        n = lax.axis_size(axis)
        even = lax.axis_index(axis) % 2 == 0

        def meet(face, start):
            pairs = [(i, i + 1) for i in range(start, n - 1, 2)]
            return lax.ppermute(face, axis, pairs + [(j, i) for i, j in pairs])

        first = meet(jnp.where(even, high_face, low_face), 0)
        second = meet(jnp.where(even, low_face, high_face), 1)
        return jnp.where(even, second, first), jnp.where(even, first, second)

    low_x, high_x = swap(melt[:, :size_y, :], melt[:, -size_y:, :], "brick")
    low_z, high_z = swap(melt[:, :, 0], melt[:, :, -1], "sec")
    return low_x, high_x, low_z[:, :, None], high_z[:, :, None]


def run_steps(got, melt, halo, slope, partition, rate, size_y):
    comps, columns, size_z = melt.shape
    size_x = columns // size_y
    slots = got.shape[0] // SEND
    sums = shape(comps * size_y, size_x * size_z)
    return kernel_call(
        steps_kernel,
        (
            shape(slots * BACK, LANES),
            shape(comps, columns, size_z),
            sums,
            shape(slots // GROUP * 5 // 8, comps + 1, GROUP, LANES),
        ),
        [SMEM, SMEM, SMEM] + [VMEM] * 6,
        (VMEM, VMEM, VMEM, VMEM),
        [
            pltpu.VMEM((PAIRS, columns, size_z), jnp.int32),
            pltpu.VMEM((columns, size_z), jnp.float32),
            pltpu.VMEM((comps * size_y, size_x * size_z), jnp.bfloat16),
            pltpu.VMEM((comps, GROUP, LANES), jnp.float32),
        ],
    )(slope, partition, rate, got, melt, *halo)


def run_kept(kept, before, dims):
    return kernel_call(
        functools.partial(kept_kernel, dims),
        shape(*before.shape),
        [VMEM] * 2,
        VMEM,
        cost=8_000_000_000,
    )(kept, before)


def exchange(rows, devices):
    each = rows.shape[0] // CAP
    swapped = lax.all_to_all(
        rows.reshape(each, CAP, LANES), AXES, split_axis=0, concat_axis=0, tiled=True
    )
    return swapped.reshape(rows.shape)


def local(melt, velocity, radius, cell, target, count, slope, partition, rate):
    devices = lax.axis_size(AXES)
    size_x, size_y, comps, size_z = melt.shape
    blocks = target.shape[0]
    slots = devices * CAP
    sent, slot_of = kernel_call(
        pack_kernel,
        (shape(slots * SEND, LANES), jax.ShapeDtypeStruct((blocks,), jnp.int32)),
        [HBM] * 5,
        (VMEM, SMEM),
        [
            pltpu.SMEM((blocks,), jnp.int32),
            pltpu.SMEM((blocks,), jnp.int32),
            pltpu.VMEM((3, blocks, LANES), jnp.float32),
            pltpu.VMEM((blocks, LANES), jnp.float32),
            pltpu.VMEM((blocks, LANES), jnp.int32),
            pltpu.SMEM((devices,), jnp.int32),
            pltpu.SemaphoreType.DMA((5,)),
        ],
        limit=WHOLE,
    )(target, count, jnp.transpose(velocity, (1, 0, 2)), radius, cell)
    got = exchange(sent, devices)
    start = jnp.transpose(melt, (2, 0, 1, 3)).reshape(comps, size_x * size_y, size_z)
    halo = neighbours(start, size_y)
    back, middle, acc, kept = run_steps(got, start, halo, slope, partition, rate, size_y)
    returned = exchange(back, devices)
    halo = neighbours(middle, size_y)
    acc = run_kept(kept, acc, (size_x, size_y, size_z))
    final = kernel_call(
        finish_kernel,
        shape(size_x, comps, size_y, size_z),
        [SMEM] + [VMEM] * 6,
        VMEM,
    )(rate, middle, acc, *halo)
    melt_out = jnp.transpose(final, (0, 2, 1, 3))
    velocity_out, radius_out = kernel_call(
        unpack_kernel,
        (shape(3, blocks, LANES), shape(blocks, LANES)),
        [SMEM, VMEM],
        (HBM, HBM),
        [
            pltpu.VMEM((3, blocks, LANES), jnp.float32),
            pltpu.VMEM((blocks, LANES), jnp.float32),
            pltpu.SemaphoreType.DMA((8,)),
        ],
    )(slot_of, returned)
    return melt_out, jnp.transpose(velocity_out, (1, 0, 2)), radius_out


def solution(mesh):
    return jax.shard_map(
        local,
        mesh=mesh,
        in_specs=(
            P("brick", None, None, "sec"),
            P(AXES, None, None),
            P(AXES, None),
            P(AXES, None),
            P(AXES),
            P(AXES),
            P(),
            P(),
            P(),
        ),
        out_specs=(P("brick", None, None, "sec"), P(AXES, None, None), P(AXES, None)),
        check_vma=False,
    )
```
